256 devices in a mesh: region: 8 (over y, x_hi), blk: 32 (over x_lo, z, core).
Axes of the slice: x: 4 (x_hi: 2, x_lo: 2; x = x_hi * 2 + x_lo), y: 4, z: 8, core: 2. Of those that a mesh axis runs over, the one named last changes fastest.
Arguments:
- incident: bfloat16 [8, 8, 256, 32, 128], P(None, 'region', 'blk'), may hold values from -6 to 6
- past_currents: bfloat16 [4, 8, 256, 32, 128], P(None, 'region', 'blk'), may hold values from -6 to 6
- self_inverse: bfloat16 [8, 256, 128, 128], P('region', 'blk'), may hold values from -0.5 to 0.5
- near_tiles: bfloat16 [8, 256, 32, 128, 128], P('region', 'blk'), may hold values from -0.046875 to 0.046875
- near_cols: int32 [8, 256, 32], P('region', 'blk'), may hold values from 0 to 255, as said below
- near_delay: int32 [8, 256, 32], P('region', 'blk'), may hold values from 1 to 4
- block_slot: int32 [8, 256], P('region'), may hold values from 0 to 255, as said below
- far_out: bfloat16 [8, 256, 128, 64], P('region', 'blk'), may hold values from -0.015625 to 0.015625
- far_in: bfloat16 [8, 256, 64, 128], P('region', 'blk'), may hold values from -0.75 to 0.75
- far_pairs: int32 [8, 7], P('region'), may hold values from 0 to 7, as said below
- far_delay: int32 [8, 7], P('region'), may hold values from 1 to 4
- far_coupling: float32 [8, 7, 64, 64], P('region'), may hold values from -0.25 to 0.25
Outputs:
- currents: bfloat16 [8, 8, 256, 32, 128], P(None, 'region', 'blk')
The draws below stay inside these ranges and needn't reach their ends.
Inputs may be any that keep to these rules, and one draw needn't show every extreme that they name: `block_slot`: each region's ids are a permutation of 0 to 255. `near_cols`: for block row at position b, every near source block is stored on a blk device at most 4 devices from the device of b, and the first tile of every row lies exactly 4 devices away. `far_pairs`: region g lists each of the other 7 regions exactly once.
All inputs are finite; a program needn't handle non-finite values.
Results may differ from the reference program's by a relative error of at most 0.01.
Values may be sent and summed in bfloat16 or wider, within the bound.
No kernel may reach another device: no remote copies, remote signals or barrier semaphores. Data moves between devices by JAX's collectives and lax.ppermute only.
A program may use at most 64 MiB of HBM per device.

```python
import jax
import jax.numpy as jnp
from jax import lax

ROWS = 128
PULSES = 32
RANK = 64
BLK_DEV = 8
NEAR = 32
STEPS = 8
DMAX = 4
REACH = 4
REGIONS = 8
GB = 256
FARP = 7


def layout(key):
    base = jax.random.fold_in(key, 7)
    keys = jax.random.split(base, 3)
    slots = jax.vmap(lambda inner: jax.random.permutation(inner, GB))(jax.random.split(keys[0], REGIONS)).astype(jnp.int32)
    devices = GB // BLK_DEV
    home = (jnp.arange(GB, dtype=jnp.int32) // BLK_DEV)[None, :, None]
    offsets = jax.random.randint(keys[1], (REGIONS, GB, NEAR), -REACH, REACH + 1)
    edge = jnp.where(home + REACH < devices, REACH, -REACH)
    offsets = jnp.concatenate([jnp.broadcast_to(edge, (REGIONS, GB, 1)), offsets[:, :, 1:]], axis=2)
    target_dev = jnp.clip(home + offsets, 0, devices - 1)
    within = jax.random.randint(keys[2], (REGIONS, GB, NEAR), 0, BLK_DEV)
    target = (target_dev * BLK_DEV + within).astype(jnp.int32)
    inverse = jnp.argsort(slots, axis=1, stable=True).astype(jnp.int32)
    ids = jnp.take_along_axis(inverse, target.reshape(REGIONS, -1), axis=1).reshape(REGIONS, GB, NEAR)
    return (slots, ids.astype(jnp.int32))


def draw_block_slot(key, part):
    return layout(key)[0]


def draw_near_cols(key, part):
    return layout(key)[1]


def draw_far_pairs(key, part):
    base = jax.random.fold_in(key, 13)
    others = jax.vmap(lambda inner: jax.random.permutation(inner, REGIONS - 1))(jax.random.split(base, REGIONS)).astype(jnp.int32)
    owner = jnp.arange(REGIONS, dtype=jnp.int32)[:, None]
    return (others + (others >= owner).astype(jnp.int32)).astype(jnp.int32)


def set_ends(array, rng, low, largest):
    spot = [jax.random.randint(jax.random.fold_in(rng, axis), (), 0, length) for axis, length in enumerate(array.shape)]
    longest = array.shape.index(max(array.shape))
    beside = spot[:longest] + [(spot[longest] + 1) % array.shape[longest]] + spot[longest + 1:]
    return array.at[tuple(spot)].set(low).at[tuple(beside)].set(largest)


def level_of(rng, extent, shards, smallest, top_value):
    def one(axis_at, parts):
        steps = jax.random.uniform(jax.random.fold_in(jax.random.fold_in(rng, 6), axis_at), (parts,), jnp.float32, smallest / len(shards), top_value / len(shards))
        return jnp.repeat(jnp.exp(steps), extent[axis_at] // parts).reshape((-1,) + (1,) * (len(extent) - axis_at - 1))

    level = one(*shards[0])
    for cut in shards[1:]:
        level = level * one(*cut)
    return level


def normal_values(own_key, dims, spread, most, cuts=(), held_as=jnp.bfloat16):
    factor_of = level_of(own_key, dims, cuts, -0.22, 0.18) if cuts else 1.0
    entries = jax.random.normal(own_key, dims, jnp.float32) * spread * factor_of
    return jnp.minimum(jnp.maximum(entries, -most), most).astype(held_as)


def setup_inputs(seed: int = 0) -> dict:
    arg_keys = jax.random.split(jax.random.key(seed), 13)
    return {
        "incident": normal_values(arg_keys[0], (STEPS, REGIONS, GB, PULSES, ROWS), 1.0, 6.0, ((1, 8), (2, 32))),
        "past_currents": normal_values(arg_keys[1], (DMAX, REGIONS, GB, PULSES, ROWS), 1.0, 6.0, ((1, 8), (2, 32))),
        "self_inverse": normal_values(arg_keys[2], (REGIONS, GB, ROWS, ROWS), ROWS ** -0.5, 0.5, ((0, 8), (1, 32))),
        "near_tiles": normal_values(arg_keys[3], (REGIONS, GB, NEAR, ROWS, ROWS), (4 * ROWS * NEAR) ** -0.5, 0.046875, ((0, 8), (1, 32))),
        "near_cols": draw_near_cols(jax.random.fold_in(arg_keys[12], 71), 0),
        "near_delay": set_ends(jax.random.randint(arg_keys[5], (REGIONS, GB, NEAR), 1, DMAX + 1), jax.random.fold_in(arg_keys[5], 1), 1, DMAX).astype(jnp.int32),
        "block_slot": draw_block_slot(jax.random.fold_in(arg_keys[12], 71), 0),
        "far_out": normal_values(arg_keys[7], (REGIONS, GB, ROWS, RANK), (4 * ROWS * GB) ** -0.5, 0.015625, ((0, 8), (1, 32))),
        "far_in": normal_values(arg_keys[8], (REGIONS, GB, RANK, ROWS), RANK ** -0.5, 0.75, ((0, 8), (1, 32))),
        "far_pairs": draw_far_pairs(jax.random.fold_in(arg_keys[12], 71), 0),
        "far_delay": set_ends(jax.random.randint(arg_keys[10], (REGIONS, FARP), 1, DMAX + 1), jax.random.fold_in(arg_keys[10], 1), 1, DMAX).astype(jnp.int32),
        "far_coupling": normal_values(arg_keys[11], (REGIONS, FARP, RANK, RANK), (RANK * FARP) ** -0.5, 0.25, ((0, 8),), jnp.float32),
    }


def moments(current, far_out):
    return jnp.einsum('gbpr,gbrk->gpk', current.astype(jnp.float32), far_out.astype(jnp.float32))


def near_region(packed):
    history, tiles, position, delays = packed
    sources = history[delays - 1, position]
    return jnp.einsum('bjpk,bjkm->bpm', sources.astype(jnp.float32), tiles.astype(jnp.float32))


def reference(incident, past_currents, self_inverse, near_tiles, near_cols, near_delay, block_slot, far_out, far_in, far_pairs, far_delay, far_coupling):
    regions = block_slot.shape[0]
    position = jnp.take_along_axis(block_slot, near_cols.reshape(regions, -1), axis=1).reshape(near_cols.shape).astype(jnp.int32)
    history = past_currents
    moment_hist = jnp.stack([moments(past_currents[k], far_out) for k in range(DMAX)])
    outputs = []
    for step in range(STEPS):
        sources = moment_hist[far_delay - 1, far_pairs]
        blended = jnp.einsum('gfpk,gfkl->gpl', sources, far_coupling, precision=lax.Precision.HIGHEST).astype(jnp.bfloat16)
        far_field = jnp.einsum('gpk,gbkr->gbpr', blended.astype(jnp.float32), far_in.astype(jnp.float32))
        near_field = lax.map(near_region, (jnp.moveaxis(history, 1, 0), near_tiles, position, near_delay))
        driven = (incident[step].astype(jnp.float32) - near_field - far_field).astype(jnp.bfloat16)
        current = jnp.einsum('gbpk,gbkm->gbpm', driven.astype(jnp.float32), self_inverse.astype(jnp.float32)).astype(jnp.bfloat16)
        outputs.append(current)
        history = jnp.concatenate([current[None], history[:-1]], axis=0)
        moment_hist = jnp.concatenate([moments(current, far_out)[None], moment_hist[:-1]], axis=0)
    return jnp.stack(outputs)
```

```python
import functools

import jax
import jax.numpy as jnp
from jax import lax
from jax.experimental import pallas as pl
from jax.experimental.pallas import tpu as pltpu
from jax.sharding import PartitionSpec as P

SPAN = 2
VMEM_LIMIT = 12 * 2**20
F32 = jnp.float32
BF16 = jnp.bfloat16


def dot(a, b):
    return jnp.dot(a, b, preferred_element_type=F32)


def in_vmem(x):
    return pltpu.with_memory_space_constraint(x, pltpu.VMEM)


def call(kernel, out_shape, vmem_args, smem_args=(), scratch=(), aliases=None, flops=0):
    specs = [pl.BlockSpec(memory_space=pltpu.SMEM)] * len(smem_args)
    specs += [pl.BlockSpec(memory_space=pltpu.VMEM)] * len(vmem_args)
    return pl.pallas_call(
        kernel,
        out_shape=out_shape,
        in_specs=specs,
        out_specs=jax.tree.map(lambda _: pl.BlockSpec(memory_space=pltpu.VMEM), out_shape),
        scratch_shapes=list(scratch),
        input_output_aliases=aliases or {},
        compiler_params=pltpu.CompilerParams(vmem_limit_bytes=VMEM_LIMIT),
        cost_estimate=pl.CostEstimate(flops=flops, bytes_accessed=1 << 20, transcendentals=0),
    )(*smem_args, *vmem_args)


def shape(dims, dtype):
    return jax.ShapeDtypeStruct(dims, dtype)


def swap_cores(value):
    n = lax.axis_size("blk")
    return lax.ppermute(value, "blk", [(i, i ^ 1) for i in range(n)])


def paired(value, wanted, by):
    chips = lax.axis_size("blk") // 2
    pairs = []
    for c in range(chips - by):
        if wanted(c):
            for core in range(2):
                low, high = 2 * c + core, 2 * (c + by) + core
                pairs += [(low, high), (high, low)]
    return lax.ppermute(value, "blk", pairs)


def window(value):
    direct = [
        value,
        paired(value, lambda c: c % 2 == 1, 1),
        paired(value, lambda c: c % 4 >= 2, 2),
        paired(value, lambda c: c % 2 == 0, 1),
        paired(value, lambda c: c % 4 < 2, 2),
    ]
    return direct + [swap_cores(v) for v in direct]


def piece_offsets(device, blocks):
    chip, core = device // 2, device % 2
    one = jnp.where(chip % 2 == 1, 1, -1)
    two = jnp.where(chip % 4 >= 2, 2, -2)
    rel = jnp.stack([jnp.zeros_like(one), one, two, -one, -two]) + SPAN
    return (jnp.concatenate([rel * 2 + core, rel * 2 + 1 - core]) * blocks).astype(jnp.int32)


def start_kernel(pair_ref, delay_ref, past_ref, fin_ref, sinv_ref, fout_ref, coup_ref, pay_ref, mom_ref, send_ref):
    depth, blocks, pulses, _ = past_ref.shape
    rank = fin_ref.shape[1]
    farp = coup_ref.shape[0]
    for p in range(8):
        if p < farp:
            slab = coup_ref[p].astype(BF16)
        elif p == 7:
            row = lax.broadcasted_iota(jnp.int32, (rank, rank), 0)
            lane = lax.broadcasted_iota(jnp.int32, (rank, rank), 1)
            ints = jnp.zeros((rank, rank), jnp.int32)
            for q in range(farp):
                number = jnp.where(row == 0, pair_ref[0, q], jnp.where(row == 1, delay_ref[0, q], 0))
                ints = ints + jnp.where(lane == q, number, 0)
            slab = ints.astype(F32).astype(BF16)
        else:
            slab = jnp.zeros((rank, rank), BF16)
        at, side = (p % 4) * rank, (p // 4) * rank
        for g in range(send_ref.shape[0]):
            send_ref[g, at : at + rank, side : side + rank] = slab
    total = jnp.zeros(mom_ref.shape, F32)
    for b in range(blocks):
        response = dot(fin_ref[b], sinv_ref[b]).astype(BF16)
        rows = [past_ref[0, b], response] + [past_ref[k, b] for k in range(1, depth)]
        whole = jnp.concatenate(rows, axis=0)
        pay_ref[b] = whole
        total = total + dot(whole, fout_ref[b])
    mom_ref[...] = total


def step_kernel(step, last, packs, *refs):
    refs = list(refs)
    code_ref, off_ref = refs[:2]
    pieces = refs[2:12]
    tiles_ref, inc_ref, sinv_ref, fout_ref = refs[12:16]
    rest = refs[16:]
    moms = []
    if step > 0:
        rest = rest[1:]
    if packs:
        moms, rest = rest[:packs], rest[packs:]
    blocks, near = tiles_ref.shape[:2]
    pulses = inc_ref.shape[2]
    if last:
        loc_ref, hist_ref = rest
        rows = pulses
    else:
        hist_ref, pay_ref, loc_ref, mom_ref = rest[:4]
        rows = pay_ref.shape[1]
    per_time = hist_ref.shape[0] // 4
    held = hist_ref.shape[1]

    if step == 0:
        for k in range(1, 4):
            hist_ref[pl.ds((3 - k) * per_time, per_time), pulses:held, :] = jnp.zeros(
                (per_time, held - pulses, hist_ref.shape[2]), BF16
            )
    for i, piece in enumerate(pieces):
        off = off_ref[i]
        if step == 0:
            hist_ref[pl.ds(3 * per_time + off, blocks), :, :] = piece[:, :held, :]
            for k in range(1, 4):
                row = held + (k - 1) * pulses
                hist_ref[pl.ds((3 - k) * per_time + off, blocks), :pulses, :] = piece[:, row : row + pulses, :]
        else:
            hist_ref[pl.ds(((step - 1) % 4) * per_time + off, blocks), :rows, :] = piece[...]

    def source(at):
        code = code_ref[at]
        slot = (step - (code & 7)) & 3
        return hist_ref[slot * per_time + (code >> 3), :rows, :]

    def row(b, total):
        acc = jnp.zeros((rows, tiles_ref.shape[3]), F32)
        for j in range(0, near, 2):
            at = b * near + j
            both = jnp.concatenate([source(at), source(at + 1)], axis=1)
            tile = tiles_ref[b, j : j + 2].reshape(-1, tiles_ref.shape[3])
            acc = acc + dot(both, tile)
        main = inc_ref[step, b].astype(F32) - acc[:pulses]
        driven = main if last else jnp.concatenate([main, -acc[pulses:]], axis=0)
        current = dot(driven.astype(BF16), sinv_ref[b])
        loc_ref[b] = current[:pulses]
        if last:
            return total
        rounded = current.astype(BF16)
        pay_ref[b] = rounded
        return total + dot(rounded, fout_ref[b])

    total = lax.fori_loop(0, blocks, row, jnp.zeros((rows, fout_ref.shape[2]), F32))
    if last:
        return
    if not packs:
        mom_ref[...] = total
        return
    main_ref = rest[4]
    main_ref[...] = pay_ref[:, :pulses, :]
    listed = [m[...] for m in moms] + [total[:pulses]]
    every = jnp.concatenate(listed, axis=0).astype(BF16)
    half, rank = every.shape[0] // 2, every.shape[1]
    mom_ref[:half, :rank] = every[:half]
    mom_ref[:half, rank:] = every[half:]
    mom_ref[half:, :] = jnp.zeros((mom_ref.shape[0] - half, mom_ref.shape[1]), BF16)


def sum_kernel(in_ref, out_ref):
    total = in_ref[0].astype(F32)
    for i in range(1, in_ref.shape[0]):
        total = total + in_ref[i].astype(F32)
    for i in range(out_ref.shape[0]):
        out_ref[i] = total.astype(BF16)


def copies_kernel(in_ref, out_ref):
    for i in range(out_ref.shape[0]):
        out_ref[i] = in_ref[...]


def finish_kernel(steps, pair_ref, delay_ref, own_ref, got_ref, coup_ref, *refs):
    pays = refs[:steps]
    locs = refs[steps : 2 * steps]
    out_ref, low_ref, high_ref, qrev_ref, c_ref, bl_ref, a_ref = refs[2 * steps :]
    regions, farp = pair_ref.shape
    depth = 4
    pulses = locs[0].shape[1]
    rank = coup_ref.shape[2] // 2
    chunk = got_ref.shape[2]
    blocks = locs[0].shape[0]
    held = pulses + rank
    first = held + (depth - 1) * pulses
    half = (first + (steps - 2) * held + pulses) // 2

    def rows_of(g, at, count):
        parts = []
        for r in range(at, at + count, 16):
            side, row = divmod(r, half)
            parts.append(
                got_ref[row // chunk, g, row % chunk : row % chunk + 16, side * rank : (side + 1) * rank]
            )
        return jnp.concatenate(parts, axis=0)

    def keep(time, g, value):
        low_ref[(time + depth) * regions + g, :, :rank] = value
        high_ref[(time + depth) * regions + g, :, rank:] = value

    low_ref[...] = jnp.zeros(low_ref.shape, BF16)
    high_ref[...] = jnp.zeros(high_ref.shape, BF16)
    bl_ref[...] = jnp.zeros(bl_ref.shape, BF16)
    a_ref[...] = jnp.zeros(a_ref.shape, BF16)
    for g in range(regions):
        keep(-1, g, rows_of(g, 0, pulses))
        for k in range(1, depth):
            keep(-1 - k, g, rows_of(g, held + (k - 1) * pulses, pulses))
        for lag in range(steps - 1):
            at = pulses if lag == 0 else first + (lag - 1) * held + pulses
            spot = (steps - 2 - lag) * rank
            qrev_ref[g, spot : spot + rank, :] = rows_of(g, at, rank)
        qrev_ref[g, (steps - 1) * rank :, :] = jnp.zeros((rank, rank), BF16)
        for p in range(8):
            c_ref[g, p * rank : (p + 1) * rank, :] = (
                coup_ref[g, (p % 4) * rank : (p % 4 + 1) * rank, (p // 4) * rank : (p // 4 + 1) * rank]
                if p < farp
                else jnp.zeros((rank, rank), BF16)
            )

    for n in range(steps):
        blended = []
        for g in range(regions):
            acc = jnp.zeros((pulses, rank), F32)
            for p in range(0, farp, 4):
                lanes = []
                for q in range(p, min(p + 4, farp), 2):
                    part = low_ref[(n - delay_ref[g, q] + depth) * regions + pair_ref[g, q]]
                    if q + 1 < farp:
                        part = part + high_ref[(n - delay_ref[g, q + 1] + depth) * regions + pair_ref[g, q + 1]]
                    lanes.append(part)
                lhs = jnp.concatenate(lanes, axis=1)
                acc = acc + dot(lhs, c_ref[g, p * rank : p * rank + lhs.shape[1], :])
            blended.append(acc.astype(BF16))
        for g in range(regions):
            bl_ref[g, :, n * rank : (n + 1) * rank] = blended[g]
        if n < steps - 1:
            depth_k = 2 * rank * ((n + 2) // 2)
            at = first + n * held
            spot = (steps - 2 - n) * rank
            for g in range(regions):
                change = dot(bl_ref[g, :, :depth_k], qrev_ref[g, spot : spot + depth_k, :])
                keep(n, g, (rows_of(g, at, pulses).astype(F32) - change).astype(BF16))

    mine = own_ref[0]
    for n in range(steps):
        a_ref[n * pulses : (n + 1) * pulses, (steps - 1 - n) * rank :] = bl_ref[mine, :, : (n + 1) * rank]
    for b in range(blocks):
        response = jnp.concatenate([pays[k][b, pulses : pulses + rank, :] for k in reversed(range(steps))], axis=0)
        far = dot(a_ref[...], response)
        for n in range(steps):
            out_ref[n, b] = (locs[n][b] - far[n * pulses : (n + 1) * pulses]).astype(BF16)


def on_device(
    incident,
    past_currents,
    self_inverse,
    near_tiles,
    near_cols,
    near_delay,
    block_slot,
    far_out,
    far_in,
    far_pairs,
    far_delay,
    far_coupling,
):
    steps, _, blocks, pulses, rows = incident.shape
    depth = past_currents.shape[0]
    near = near_cols.shape[2]
    ids = block_slot.shape[1]
    farp, rank = far_coupling.shape[1:3]
    regions = lax.axis_size("region")
    ring = lax.axis_size("blk")
    device = lax.axis_index("blk")
    held = pulses + rank
    near_blocks = (2 * SPAN + 1) * 2 * blocks

    match = near_cols[0][:, :, None] == jnp.arange(ids, dtype=jnp.int32)
    position = jnp.sum(jnp.where(match, block_slot[0], 0), axis=2)
    local = jnp.clip(position - (device // 2 - SPAN) * 2 * blocks, 0, near_blocks - 1)
    code = (local * 8 + near_delay[0]).reshape(-1).astype(jnp.int32)
    offsets = piece_offsets(device, blocks)

    tiles = in_vmem(near_tiles[0])
    sinv, fout, fin = self_inverse[0], far_out[0], far_in[0]
    inc = incident[:, 0]
    past = past_currents[:, 0]

    first = held + (depth - 1) * pulses
    payload, moment, coupling = call(
        start_kernel,
        (
            shape((blocks, first, rows), BF16),
            shape((first, rank), F32),
            shape((regions, 4 * rank, 2 * rank), BF16),
        ),
        [past, fin, sinv, fout, far_coupling[0]],
        [far_pairs, far_delay],
    )
    coupling = lax.all_to_all(coupling, "region", 0, 0, tiled=True)
    pairs = coupling[:, 3 * rank, rank : rank + farp].astype(jnp.int32)
    delays = coupling[:, 3 * rank + 1, rank : rank + farp].astype(jnp.int32)
    code, offsets, pairs, delays = lax.optimization_barrier((code, offsets, pairs, delays))
    pays, locs, moms = [payload], [], [moment]
    hist = None
    hist_shape = shape((4 * near_blocks, held, rows), BF16)
    flops = 2 * blocks * near * held * rows * rows
    for n in range(steps):
        last = n == steps - 1
        packs = len(moms) if n == steps - 2 else 0
        args = window(payload) + [tiles, inc, sinv, fout]
        aliases = {}
        if n > 0:
            args.append(in_vmem(hist))
            aliases = {2 + len(args) - 1: 1 if last else 0}
        loc_shape = shape((blocks, pulses, rows), F32)
        if last:
            outs = (loc_shape, hist_shape)
        elif packs:
            args += moms
            outs = (
                hist_shape,
                shape((blocks, held, rows), BF16),
                loc_shape,
                shape((512, 2 * rank), BF16),
                shape((blocks, pulses, rows), BF16),
            )
        else:
            outs = (hist_shape, shape((blocks, held, rows), BF16), loc_shape, shape((held, rank), F32))
        got = call(
            functools.partial(step_kernel, n, last, packs),
            outs,
            args,
            [code, offsets],
            aliases=aliases,
            flops=flops,
        )
        if last:
            loc = got[0]
        elif packs:
            hist, payload, loc, packed, main = got
            pays.append(payload)
            payload = main
        else:
            hist, payload, loc, moment = got
            pays.append(payload)
            moms.append(moment)
        locs.append(loc)

    chunks = packed.reshape(ring, 512 // ring, 2 * rank)
    shares = lax.all_to_all(chunks, "blk", 0, 0, tiled=True)
    spread = call(sum_kernel, shape((regions, *shares.shape[1:]), BF16), [shares])
    spread = lax.all_to_all(spread, "region", 0, 0, tiled=True)
    every = call(copies_kernel, shape((ring, *spread.shape), BF16), [spread])
    every = lax.all_to_all(every, "blk", 0, 0, tiled=True)

    own = lax.axis_index("region").astype(jnp.int32).reshape(1)
    currents = call(
        functools.partial(finish_kernel, steps),
        shape((steps, blocks, pulses, rows), BF16),
        [every, coupling, *pays, *locs],
        [pairs, delays, own],
        scratch=[
            pltpu.VMEM(((depth + steps) * regions, pulses, 2 * rank), BF16),
            pltpu.VMEM(((depth + steps) * regions, pulses, 2 * rank), BF16),
            pltpu.VMEM((regions, steps * rank, rank), BF16),
            pltpu.VMEM((regions, 8 * rank, rank), BF16),
            pltpu.VMEM((regions, pulses, steps * rank), BF16),
            pltpu.VMEM((steps * pulses, steps * rank), BF16),
        ],
    )
    return currents[:, None]


def solution(mesh):
    in_specs = (
        P(None, "region", "blk", None, None),
        P(None, "region", "blk", None, None),
        P("region", "blk", None, None),
        P("region", "blk", None, None, None),
        P("region", "blk", None),
        P("region", "blk", None),
        P("region", None),
        P("region", "blk", None, None),
        P("region", "blk", None, None),
        P("region", None),
        P("region", None),
        P("region", None, None, None),
    )
    out_specs = P(None, "region", "blk", None, None)
    return jax.shard_map(on_device, mesh=mesh, in_specs=in_specs, out_specs=out_specs, check_vma=False)
```

```python
import functools

import jax
import jax.numpy as jnp
from jax import lax
from jax.experimental import pallas as pl
from jax.experimental.pallas import tpu as pltpu
from jax.sharding import PartitionSpec as P

SPAN = 2
VMEM_LIMIT = 12 * 2**20
F32 = jnp.float32
BF16 = jnp.bfloat16


def dot(a, b):
    return jnp.dot(a, b, preferred_element_type=F32)


def in_vmem(x):
    return pltpu.with_memory_space_constraint(x, pltpu.VMEM)


def in_hbm(x):
    return pltpu.with_memory_space_constraint(x, pltpu.HBM)


def call(kernel, out_shape, vmem_args, smem_args=(), scratch=(), aliases=None, flops=0, fetch=False):
    specs = [pl.BlockSpec(memory_space=pltpu.SMEM)] * len(smem_args)
    for arg in vmem_args:
        if fetch:
            specs.append(pl.BlockSpec(arg.shape, lambda i, n=arg.ndim: (0,) * n))
        else:
            specs.append(pl.BlockSpec(memory_space=pltpu.VMEM))
    return pl.pallas_call(
        kernel,
        grid=(1,) if fetch else (),
        out_shape=out_shape,
        in_specs=specs,
        out_specs=jax.tree.map(lambda _: pl.BlockSpec(memory_space=pltpu.VMEM), out_shape),
        scratch_shapes=list(scratch),
        input_output_aliases=aliases or {},
        compiler_params=pltpu.CompilerParams(vmem_limit_bytes=VMEM_LIMIT),
        cost_estimate=pl.CostEstimate(flops=flops, bytes_accessed=1 << 20, transcendentals=0),
    )(*smem_args, *vmem_args)


def shape(dims, dtype):
    return jax.ShapeDtypeStruct(dims, dtype)


def swap_cores(value):
    n = lax.axis_size("blk")
    return lax.ppermute(value, "blk", [(i, i ^ 1) for i in range(n)])


def paired(value, wanted, by):
    chips = lax.axis_size("blk") // 2
    pairs = []
    for c in range(chips - by):
        if wanted(c):
            for core in range(2):
                low, high = 2 * c + core, 2 * (c + by) + core
                pairs += [(low, high), (high, low)]
    return lax.ppermute(value, "blk", pairs)


def window(value):
    direct = [
        value,
        paired(value, lambda c: c % 2 == 0, 1),
        paired(value, lambda c: c % 4 < 2, 2),
        paired(value, lambda c: c % 2 == 1, 1),
        paired(value, lambda c: c % 4 >= 2, 2),
    ]
    return direct + [swap_cores(v) for v in direct]


def index_kernel(device_ref, cols_ref, delay_ref, slot_ref, *refs):
    count = (len(refs) - 3) // 2
    code_ref, off_ref = refs[count : count + 2]
    sems = refs[-1]
    copies = [pltpu.make_async_copy(refs[i], refs[count + 2 + i], sems.at[i]) for i in range(count)]
    for copy in copies:
        copy.start()
    blocks, near = cols_ref.shape
    chip, core = device_ref[0] // 2, device_ref[0] % 2
    base = (chip - SPAN) * 2 * blocks
    top = (2 * SPAN + 1) * 2 * blocks - 1

    def one(at, _):
        b, j = at // near, at % near
        local = jnp.clip(slot_ref[0, cols_ref[b, j]] - base, 0, top)
        code_ref[at] = local * 8 + delay_ref[b, j]
        return 0

    lax.fori_loop(0, blocks * near, one, 0, unroll=8)
    odd = jnp.where(chip % 2 == 0, 1, -1)
    two = jnp.where(chip % 4 < 2, 2, -2)
    for i, rel in enumerate((0, odd, two, -odd, -two)):
        off_ref[i] = ((rel + SPAN) * 2 + core) * blocks
        off_ref[i + 5] = ((rel + SPAN) * 2 + 1 - core) * blocks
    for copy in copies:
        copy.wait()


def start_kernel(past_ref, fin_ref, sinv_ref, fout_ref, coup_ref, pair_ref, delay_ref, pay_ref, mom_ref, send_ref):
    depth, blocks, pulses, _ = past_ref.shape
    rank = fin_ref.shape[1]
    farp = coup_ref.shape[0]
    for p in range(8):
        if p < farp:
            slab = coup_ref[p].astype(BF16)
        elif p == 7:
            row = lax.broadcasted_iota(jnp.int32, (rank, rank), 0)
            rest = jnp.zeros((1, rank - farp), jnp.int32)
            pair, delay = (jnp.concatenate([ref[...], rest], axis=1) for ref in (pair_ref, delay_ref))
            ints = jnp.where(row == 0, pair, jnp.where(row == 1, delay, 0))
            slab = ints.astype(F32).astype(BF16)
        else:
            slab = jnp.zeros((rank, rank), BF16)
        at, side = (p % 4) * rank, (p // 4) * rank
        for g in range(send_ref.shape[0]):
            send_ref[g, at : at + rank, side : side + rank] = slab
    total = jnp.zeros(mom_ref.shape, F32)
    for b in range(blocks):
        response = dot(fin_ref[b], sinv_ref[b]).astype(BF16)
        rows = [past_ref[0, b], response] + [past_ref[k, b] for k in range(1, depth)]
        whole = jnp.concatenate(rows, axis=0)
        pay_ref[b] = whole
        total = total + dot(whole, fout_ref[b])
    mom_ref[...] = total


def step_kernel(step, last, packs, *refs):
    refs = list(refs)
    code_ref, off_ref = refs[:2]
    pieces = refs[2:12]
    tiles_ref, inc_ref, sinv_ref, fout_ref = refs[12:16]
    rest = refs[16:]
    moms = []
    if step > 0:
        rest = rest[1:]
    if packs:
        moms, rest = rest[:packs], rest[packs:]
    blocks, near = tiles_ref.shape[:2]
    pulses = inc_ref.shape[2]
    if last:
        loc_ref, hist_ref = rest
        rows = pulses
    else:
        hist_ref, pay_ref, mom_ref = rest[:3]
        rows = pay_ref.shape[1]
    per_time = hist_ref.shape[0] // 4
    held = hist_ref.shape[1]

    if step == 0:
        for k in range(1, 4):
            hist_ref[pl.ds((3 - k) * per_time, per_time), pulses:held, :] = jnp.zeros(
                (per_time, held - pulses, hist_ref.shape[2]), BF16
            )
    for i, piece in enumerate(pieces):
        off = off_ref[i]
        if step == 0:
            hist_ref[pl.ds(3 * per_time + off, blocks), :, :] = piece[:, :held, :]
            for k in range(1, 4):
                row = held + (k - 1) * pulses
                hist_ref[pl.ds((3 - k) * per_time + off, blocks), :pulses, :] = piece[:, row : row + pulses, :]
        else:
            hist_ref[pl.ds(((step - 1) % 4) * per_time + off, blocks), :rows, :] = piece[...]

    def source(at):
        code = code_ref[at]
        slot = (step - (code & 7)) & 3
        return hist_ref[slot * per_time + (code >> 3), :rows, :]

    def row(b, total):
        acc = jnp.zeros((rows, tiles_ref.shape[3]), F32)
        for j in range(0, near, 2):
            at = b * near + j
            both = jnp.concatenate([source(at), source(at + 1)], axis=1)
            tile = tiles_ref[b, j : j + 2].reshape(-1, tiles_ref.shape[3])
            acc = acc + dot(both, tile)
        main = inc_ref[step, b].astype(F32) - acc[:pulses]
        driven = main if last else jnp.concatenate([main, -acc[pulses:]], axis=0)
        current = dot(driven.astype(BF16), sinv_ref[b])
        if last:
            loc_ref[b] = current
            return total
        rounded = current.astype(BF16)
        pay_ref[b] = rounded
        return total + dot(rounded, fout_ref[b])

    total = lax.fori_loop(0, blocks, row, jnp.zeros((rows, fout_ref.shape[2]), F32))
    if last:
        return
    if not packs:
        mom_ref[...] = total
        return
    main_ref = rest[3]
    main_ref[...] = pay_ref[:, :pulses, :]
    listed = [m[...] for m in moms] + [total[:pulses]]
    every = jnp.concatenate(listed, axis=0).astype(BF16)
    half, rank = every.shape[0] // 2, every.shape[1]
    mom_ref[:half, :rank] = every[:half]
    mom_ref[:half, rank:] = every[half:]
    mom_ref[half:, :] = jnp.zeros((mom_ref.shape[0] - half, mom_ref.shape[1]), BF16)


def sum_kernel(in_ref, out_ref):
    total = in_ref[0].astype(F32)
    for i in range(1, in_ref.shape[0]):
        total = total + in_ref[i].astype(F32)
    for i in range(out_ref.shape[0]):
        out_ref[i] = total.astype(BF16)


def copies_kernel(in_ref, out_ref):
    for i in range(out_ref.shape[0]):
        out_ref[i] = in_ref[...]


def finish_kernel(steps, farp, own_ref, got_ref, coup_ref, *refs):
    pays = refs[:steps]
    loc_ref, out_ref, low_ref, high_ref, qrev_ref, c_ref, bl_ref, a_ref, ints_ref, num_ref, sem = refs[steps:]
    regions = got_ref.shape[0]
    depth = 4
    blocks, pulses = loc_ref.shape[:2]
    rank = coup_ref.shape[2] // 2
    held = pulses + rank
    first = held + (depth - 1) * pulses
    half = (first + (steps - 2) * held + pulses) // 2

    ints_ref[...] = jnp.zeros(ints_ref.shape, jnp.int32)
    for g in range(regions):
        numbers = coup_ref[g, 3 * rank : 3 * rank + 16, rank:].astype(F32).astype(jnp.int32)
        ints_ref[2 * g : 2 * g + 2, :rank] = numbers[:2]
    copy = pltpu.make_async_copy(ints_ref, num_ref, sem)
    copy.start()

    def rows_of(g, at, count):
        parts = []
        for r in range(at, at + count, 16):
            side, row = divmod(r, half)
            parts.append(got_ref[g, row : row + 16, side * rank : (side + 1) * rank])
        return jnp.concatenate(parts, axis=0)

    def keep(time, g, value):
        low_ref[(time + depth) * regions + g, :, :rank] = value
        high_ref[(time + depth) * regions + g, :, rank:] = value

    def source(n, g, q):
        return (n - num_ref[2 * g + 1, q] + depth) * regions + num_ref[2 * g, q]

    low_ref[...] = jnp.zeros(low_ref.shape, BF16)
    high_ref[...] = jnp.zeros(high_ref.shape, BF16)
    bl_ref[...] = jnp.zeros(bl_ref.shape, BF16)
    a_ref[...] = jnp.zeros(a_ref.shape, BF16)
    for g in range(regions):
        keep(-1, g, rows_of(g, 0, pulses))
        for k in range(1, depth):
            keep(-1 - k, g, rows_of(g, held + (k - 1) * pulses, pulses))
        for lag in range(steps - 1):
            at = pulses if lag == 0 else first + (lag - 1) * held + pulses
            spot = (steps - 2 - lag) * rank
            qrev_ref[g, spot : spot + rank, :] = rows_of(g, at, rank)
        qrev_ref[g, (steps - 1) * rank :, :] = jnp.zeros((rank, rank), BF16)
        for p in range(8):
            c_ref[g, p * rank : (p + 1) * rank, :] = (
                coup_ref[g, (p % 4) * rank : (p % 4 + 1) * rank, (p // 4) * rank : (p // 4 + 1) * rank]
                if p < farp
                else jnp.zeros((rank, rank), BF16)
            )

    copy.wait()
    for n in range(steps):
        blended = []
        for g in range(regions):
            acc = jnp.zeros((pulses, rank), F32)
            for p in range(0, farp, 4):
                lanes = []
                for q in range(p, min(p + 4, farp), 2):
                    part = low_ref[source(n, g, q)]
                    if q + 1 < farp:
                        part = part + high_ref[source(n, g, q + 1)]
                    lanes.append(part)
                lhs = jnp.concatenate(lanes, axis=1)
                acc = acc + dot(lhs, c_ref[g, p * rank : p * rank + lhs.shape[1], :])
            blended.append(acc.astype(BF16))
        for g in range(regions):
            bl_ref[g, :, n * rank : (n + 1) * rank] = blended[g]
        if n < steps - 1:
            depth_k = 2 * rank * ((n + 2) // 2)
            at = first + n * held
            spot = (steps - 2 - n) * rank
            for g in range(regions):
                change = dot(bl_ref[g, :, :depth_k], qrev_ref[g, spot : spot + depth_k, :])
                keep(n, g, (rows_of(g, at, pulses).astype(F32) - change).astype(BF16))

    mine = own_ref[0]
    for n in range(steps):
        a_ref[n * pulses : (n + 1) * pulses, (steps - 1 - n) * rank :] = bl_ref[mine, :, : (n + 1) * rank]
    for b in range(blocks):
        response = jnp.concatenate([pays[k][b, pulses : pulses + rank, :] for k in reversed(range(steps))], axis=0)
        far = dot(a_ref[...], response)
        for n in range(steps):
            local = loc_ref[b] if n == steps - 1 else pays[n + 1][b, :pulses, :].astype(F32)
            out_ref[n, b] = (local - far[n * pulses : (n + 1) * pulses]).astype(BF16)


def on_device(
    incident,
    past_currents,
    self_inverse,
    near_tiles,
    near_cols,
    near_delay,
    block_slot,
    far_out,
    far_in,
    far_pairs,
    far_delay,
    far_coupling,
):
    steps, _, blocks, pulses, rows = incident.shape
    depth = past_currents.shape[0]
    near = near_cols.shape[2]
    farp, rank = far_coupling.shape[1:3]
    regions = lax.axis_size("region")
    ring = lax.axis_size("blk")
    device = lax.axis_index("blk")
    held = pulses + rank
    near_blocks = (2 * SPAN + 1) * 2 * blocks

    past, fin = past_currents[:, 0], far_in[0]

    first = held + (depth - 1) * pulses
    payload, moment, coupling = call(
        start_kernel,
        (
            shape((blocks, first, rows), BF16),
            shape((first, rank), F32),
            shape((regions, 4 * rank, 2 * rank), BF16),
        ),
        [in_hbm(x) for x in (past, fin, self_inverse[0], far_out[0], far_coupling[0], far_pairs, far_delay)],
        fetch=True,
    )
    coupling = lax.all_to_all(coupling, "region", 0, 0, tiled=True)
    coupling, device = lax.optimization_barrier((coupling, device))
    fetched = [near_tiles[0], incident[:, 0], self_inverse[0], far_out[0]]
    code, offsets, tiles, inc, sinv, fout = pl.pallas_call(
        index_kernel,
        out_shape=(
            shape((blocks * near,), jnp.int32),
            shape((10,), jnp.int32),
            *(shape(x.shape, x.dtype) for x in fetched),
        ),
        in_specs=[pl.BlockSpec(memory_space=pltpu.SMEM)] * 4 + [pl.BlockSpec(memory_space=pltpu.HBM)] * 4,
        out_specs=(pl.BlockSpec(memory_space=pltpu.SMEM),) * 2 + (pl.BlockSpec(memory_space=pltpu.VMEM),) * 4,
        scratch_shapes=[pltpu.SemaphoreType.DMA((4,))],
        compiler_params=pltpu.CompilerParams(vmem_limit_bytes=VMEM_LIMIT),
        cost_estimate=pl.CostEstimate(flops=0, bytes_accessed=1 << 24, transcendentals=0),
    )(
        device.astype(jnp.int32).reshape(1),
        near_cols[0],
        near_delay[0],
        block_slot,
        *(in_hbm(x) for x in fetched),
    )
    pays, moms = [payload], [moment]
    hist = None
    hist_shape = shape((4 * near_blocks, held, rows), BF16)
    flops = 2 * blocks * near * held * rows * rows
    for n in range(steps):
        last = n == steps - 1
        packs = len(moms) if n == steps - 2 else 0
        args = window(payload) + [in_vmem(tiles), inc, sinv, fout]
        aliases = {}
        if n > 0:
            args.append(in_vmem(hist))
            aliases = {2 + len(args) - 1: 1 if last else 0}
        loc_shape = shape((blocks, pulses, rows), F32)
        if last:
            outs = (loc_shape, hist_shape)
        elif packs:
            args += moms
            outs = (
                hist_shape,
                shape((blocks, held, rows), BF16),
                shape((512, 2 * rank), BF16),
                shape((blocks, pulses, rows), BF16),
            )
        else:
            outs = (hist_shape, shape((blocks, held, rows), BF16), shape((held, rank), F32))
        got = call(
            functools.partial(step_kernel, n, last, packs),
            outs,
            args,
            [code, offsets],
            aliases=aliases,
            flops=flops,
        )
        if last:
            loc = got[0]
        elif packs:
            hist, payload, packed, main = got
            pays.append(payload)
            payload = main
        else:
            hist, payload, moment = got
            pays.append(payload)
            moms.append(moment)

    packed, loc = lax.optimization_barrier((packed, loc))
    shares = lax.all_to_all(packed.reshape(ring, 512 // ring, 2 * rank), "blk", 0, 0, tiled=True)
    sums = call(sum_kernel, shape(shares.shape, BF16), [shares])
    sums = lax.all_to_all(sums, "blk", 0, 0, tiled=True).reshape(512, 2 * rank)
    every = call(copies_kernel, shape((regions, *sums.shape), BF16), [sums])
    every = lax.all_to_all(every, "region", 0, 0, tiled=True)

    own = lax.axis_index("region").astype(jnp.int32).reshape(1)
    currents = call(
        functools.partial(finish_kernel, steps, farp),
        shape((steps, blocks, pulses, rows), BF16),
        [every, coupling, *pays, loc],
        [own],
        scratch=[
            pltpu.VMEM(((depth + steps) * regions, pulses, 2 * rank), BF16),
            pltpu.VMEM(((depth + steps) * regions, pulses, 2 * rank), BF16),
            pltpu.VMEM((regions, steps * rank, rank), BF16),
            pltpu.VMEM((regions, 8 * rank, rank), BF16),
            pltpu.VMEM((regions, pulses, steps * rank), BF16),
            pltpu.VMEM((steps * pulses, steps * rank), BF16),
            pltpu.VMEM((2 * regions, 128), jnp.int32),
            pltpu.SMEM((2 * regions, 128), jnp.int32),
            pltpu.SemaphoreType.DMA,
        ],
    )
    return currents[:, None]


def solution(mesh):
    in_specs = (
        P(None, "region", "blk", None, None),
        P(None, "region", "blk", None, None),
        P("region", "blk", None, None),
        P("region", "blk", None, None, None),
        P("region", "blk", None),
        P("region", "blk", None),
        P("region", None),
        P("region", "blk", None, None),
        P("region", "blk", None, None),
        P("region", None),
        P("region", None),
        P("region", None, None, None),
    )
    out_specs = P(None, "region", "blk", None, None)
    return jax.shard_map(on_device, mesh=mesh, in_specs=in_specs, out_specs=out_specs, check_vma=False)
```

```python
import functools

import jax
import jax.numpy as jnp
from jax import lax
from jax.experimental import pallas as pl
from jax.experimental.pallas import tpu as pltpu
from jax.sharding import PartitionSpec as P

SPAN = 2
VMEM_LIMIT = 12 * 2**20
F32 = jnp.float32
BF16 = jnp.bfloat16


def dot(a, b):
    return jnp.dot(a, b, preferred_element_type=F32)


def in_vmem(x):
    return pltpu.with_memory_space_constraint(x, pltpu.VMEM)


def in_hbm(x):
    return pltpu.with_memory_space_constraint(x, pltpu.HBM)


def call(kernel, out_shape, vmem_args, smem_args=(), scratch=(), aliases=None, flops=0, fetch=False):
    specs = [pl.BlockSpec(memory_space=pltpu.SMEM)] * len(smem_args)
    for arg in vmem_args:
        if fetch:
            specs.append(pl.BlockSpec(arg.shape, lambda i, n=arg.ndim: (0,) * n))
        else:
            specs.append(pl.BlockSpec(memory_space=pltpu.VMEM))
    return pl.pallas_call(
        kernel,
        grid=(1,) if fetch else (),
        out_shape=out_shape,
        in_specs=specs,
        out_specs=jax.tree.map(lambda _: pl.BlockSpec(memory_space=pltpu.VMEM), out_shape),
        scratch_shapes=list(scratch),
        input_output_aliases=aliases or {},
        compiler_params=pltpu.CompilerParams(vmem_limit_bytes=VMEM_LIMIT),
        cost_estimate=pl.CostEstimate(flops=flops, bytes_accessed=1 << 20, transcendentals=0),
    )(*smem_args, *vmem_args)


def shape(dims, dtype):
    return jax.ShapeDtypeStruct(dims, dtype)


def swap_cores(value):
    n = lax.axis_size("blk")
    return lax.ppermute(value, "blk", [(i, i ^ 1) for i in range(n)])


def paired(value, wanted, by):
    chips = lax.axis_size("blk") // 2
    pairs = []
    for c in range(chips - by):
        if wanted(c):
            for core in range(2):
                low, high = 2 * c + core, 2 * (c + by) + core
                pairs += [(low, high), (high, low)]
    return lax.ppermute(value, "blk", pairs)


def window(value, after=None):
    direct = [
        value,
        paired(value, lambda c: c % 2 == 0, 1),
        paired(value, lambda c: c % 4 < 2, 2),
        paired(value, lambda c: c % 2 == 1, 1),
        paired(value, lambda c: c % 4 >= 2, 2),
    ]
    if after is not None:
        direct[-1], after = lax.optimization_barrier((direct[-1], after))
    return direct + [swap_cores(v) for v in direct], after


def index_kernel(device_ref, cols_ref, delay_ref, slot_ref, *refs):
    count = (len(refs) - 3) // 2
    code_ref, off_ref = refs[count : count + 2]
    sems = refs[-1]
    copies = [pltpu.make_async_copy(refs[i], refs[count + 2 + i], sems.at[i]) for i in range(count)]
    for copy in copies:
        copy.start()
    blocks, near = cols_ref.shape
    chip, core = device_ref[0] // 2, device_ref[0] % 2
    base = (chip - SPAN) * 2 * blocks
    top = (2 * SPAN + 1) * 2 * blocks - 1

    def one(at, _):
        b, j = at // near, at % near
        local = jnp.clip(slot_ref[0, cols_ref[b, j]] - base, 0, top)
        code_ref[at] = local * 8 + delay_ref[b, j]
        return 0

    lax.fori_loop(0, blocks * near, one, 0, unroll=8)
    odd = jnp.where(chip % 2 == 0, 1, -1)
    two = jnp.where(chip % 4 < 2, 2, -2)
    for i, rel in enumerate((0, odd, two, -odd, -two)):
        off_ref[i] = ((rel + SPAN) * 2 + core) * blocks
        off_ref[i + 5] = ((rel + SPAN) * 2 + 1 - core) * blocks
    for copy in copies:
        copy.wait()


def start_kernel(past_ref, fin_ref, sinv_ref, fout_ref, coup_ref, pair_ref, delay_ref, pay_ref, mom_ref, send_ref):
    depth, blocks, pulses, _ = past_ref.shape
    rank = fin_ref.shape[1]
    farp = coup_ref.shape[0]
    for p in range(8):
        if p < farp:
            slab = coup_ref[p].astype(BF16)
        elif p == 7:
            row = lax.broadcasted_iota(jnp.int32, (rank, rank), 0)
            rest = jnp.zeros((1, rank - farp), jnp.int32)
            pair, delay = (jnp.concatenate([ref[...], rest], axis=1) for ref in (pair_ref, delay_ref))
            ints = jnp.where(row == 0, pair, jnp.where(row == 1, delay, 0))
            slab = ints.astype(F32).astype(BF16)
        else:
            slab = jnp.zeros((rank, rank), BF16)
        at, side = (p % 4) * rank, (p // 4) * rank
        send_ref[at : at + rank, side : side + rank] = slab
    total = jnp.zeros(mom_ref.shape, F32)
    for b in range(blocks):
        response = dot(fin_ref[b], sinv_ref[b]).astype(BF16)
        rows = [past_ref[0, b], response] + [past_ref[k, b] for k in range(1, depth)]
        whole = jnp.concatenate(rows, axis=0)
        pay_ref[b] = whole
        total = total + dot(whole, fout_ref[b])
    mom_ref[...] = total


def step_kernel(step, last, packs, *refs):
    refs = list(refs)
    code_ref, off_ref = refs[:2]
    pieces = refs[2:12]
    tiles_ref, inc_ref, sinv_ref, fout_ref = refs[12:16]
    rest = refs[16:]
    moms = []
    if step > 0:
        rest = rest[1:]
    if packs:
        moms, rest = rest[:packs], rest[packs:]
    blocks, near = tiles_ref.shape[:2]
    pulses = inc_ref.shape[2]
    if last:
        loc_ref, hist_ref = rest
        rows = pulses
    else:
        hist_ref, pay_ref, mom_ref = rest[:3]
        rows = pay_ref.shape[1]
    per_time = hist_ref.shape[0] // 4
    held = hist_ref.shape[1]

    if step == 0:
        for k in range(1, 4):
            hist_ref[pl.ds((3 - k) * per_time, per_time), pulses:held, :] = jnp.zeros(
                (per_time, held - pulses, hist_ref.shape[2]), BF16
            )
    for i, piece in enumerate(pieces):
        off = off_ref[i]
        if step == 0:
            hist_ref[pl.ds(3 * per_time + off, blocks), :, :] = piece[:, :held, :]
            for k in range(1, 4):
                row = held + (k - 1) * pulses
                hist_ref[pl.ds((3 - k) * per_time + off, blocks), :pulses, :] = piece[:, row : row + pulses, :]
        else:
            hist_ref[pl.ds(((step - 1) % 4) * per_time + off, blocks), :rows, :] = piece[...]

    def source(at):
        code = code_ref[at]
        slot = (step - (code & 7)) & 3
        return hist_ref[slot * per_time + (code >> 3), :rows, :]

    def row(b, total):
        acc = jnp.zeros((rows, tiles_ref.shape[3]), F32)
        for j in range(0, near, 2):
            at = b * near + j
            both = jnp.concatenate([source(at), source(at + 1)], axis=1)
            tile = tiles_ref[b, j : j + 2].reshape(-1, tiles_ref.shape[3])
            acc = acc + dot(both, tile)
        main = inc_ref[step, b].astype(F32) - acc[:pulses]
        driven = main if last else jnp.concatenate([main, -acc[pulses:]], axis=0)
        current = dot(driven.astype(BF16), sinv_ref[b])
        if last:
            loc_ref[b] = current
            return total
        rounded = current.astype(BF16)
        pay_ref[b] = rounded
        return total + dot(rounded, fout_ref[b])

    total = lax.fori_loop(0, blocks, row, jnp.zeros((rows, fout_ref.shape[2]), F32))
    if last:
        return
    if not packs:
        mom_ref[...] = total
        return
    main_ref = rest[3]
    main_ref[...] = pay_ref[:, :pulses, :]
    listed = [m[...] for m in moms] + [total[:pulses]]
    every = jnp.concatenate(listed, axis=0).astype(BF16)
    half, rank = every.shape[0] // 2, every.shape[1]
    mom_ref[:half, :rank] = every[:half]
    mom_ref[:half, rank:] = every[half:]
    mom_ref[half:, :] = jnp.zeros((mom_ref.shape[0] - half, mom_ref.shape[1]), BF16)


def sum_kernel(in_ref, out_ref):
    total = in_ref[0].astype(F32)
    for i in range(1, in_ref.shape[0]):
        total = total + in_ref[i].astype(F32)
    for i in range(out_ref.shape[0]):
        out_ref[i] = total.astype(BF16)


def halves_kernel(place_ref, sums_ref, coup_ref, out_ref):
    core = place_ref[1]
    for i, ref in ((0, sums_ref), (sums_ref.shape[0] // 2, coup_ref)):
        rows = ref.shape[0] // 2
        half = ref[pl.ds(pl.multiple_of(core * rows, rows), rows), :]
        for g in range(out_ref.shape[0]):
            out_ref[g, i : i + rows, :] = half


def finish_kernel(steps, farp, place_ref, mine_ref, other_ref, *refs):
    pays = refs[:steps]
    loc_ref, out_ref, got_ref, coup_ref, low_ref, high_ref, qrev_ref, c_ref, bl_ref, a_ref, ints_ref, num_ref, sem = refs[steps:]
    regions = got_ref.shape[0]
    depth = 4
    blocks, pulses = loc_ref.shape[:2]
    rank = coup_ref.shape[2] // 2
    held = pulses + rank
    first = held + (depth - 1) * pulses
    half = (first + (steps - 2) * held + pulses) // 2

    for ref, core in ((mine_ref, place_ref[1]), (other_ref, 1 - place_ref[1])):
        for whole, at in ((got_ref, 0), (coup_ref, got_ref.shape[1] // 2)):
            rows = whole.shape[1] // 2
            whole[:, pl.ds(pl.multiple_of(core * rows, rows), rows), :] = ref[:, at : at + rows, :]

    ints_ref[...] = jnp.zeros(ints_ref.shape, jnp.int32)
    for g in range(regions):
        numbers = coup_ref[g, 3 * rank : 3 * rank + 16, rank:].astype(F32).astype(jnp.int32)
        ints_ref[2 * g : 2 * g + 2, :rank] = numbers[:2]
    copy = pltpu.make_async_copy(ints_ref, num_ref, sem)
    copy.start()

    def rows_of(g, at, count):
        parts = []
        for r in range(at, at + count, 16):
            side, row = divmod(r, half)
            parts.append(got_ref[g, row : row + 16, side * rank : (side + 1) * rank])
        return jnp.concatenate(parts, axis=0)

    def keep(time, g, value):
        low_ref[(time + depth) * regions + g, :, :rank] = value
        high_ref[(time + depth) * regions + g, :, rank:] = value

    def source(n, g, q):
        return (n - num_ref[2 * g + 1, q] + depth) * regions + num_ref[2 * g, q]

    low_ref[...] = jnp.zeros(low_ref.shape, BF16)
    high_ref[...] = jnp.zeros(high_ref.shape, BF16)
    bl_ref[...] = jnp.zeros(bl_ref.shape, BF16)
    a_ref[...] = jnp.zeros(a_ref.shape, BF16)
    for g in range(regions):
        keep(-1, g, rows_of(g, 0, pulses))
        for k in range(1, depth):
            keep(-1 - k, g, rows_of(g, held + (k - 1) * pulses, pulses))
        for lag in range(steps - 1):
            at = pulses if lag == 0 else first + (lag - 1) * held + pulses
            spot = (steps - 2 - lag) * rank
            qrev_ref[g, spot : spot + rank, :] = rows_of(g, at, rank)
        qrev_ref[g, (steps - 1) * rank :, :] = jnp.zeros((rank, rank), BF16)
        for p in range(8):
            c_ref[g, p * rank : (p + 1) * rank, :] = (
                coup_ref[g, (p % 4) * rank : (p % 4 + 1) * rank, (p // 4) * rank : (p // 4 + 1) * rank]
                if p < farp
                else jnp.zeros((rank, rank), BF16)
            )

    copy.wait()
    for n in range(steps):
        blended = []
        for g in range(regions):
            acc = jnp.zeros((pulses, rank), F32)
            for p in range(0, farp, 4):
                lanes = []
                for q in range(p, min(p + 4, farp), 2):
                    part = low_ref[source(n, g, q)]
                    if q + 1 < farp:
                        part = part + high_ref[source(n, g, q + 1)]
                    lanes.append(part)
                lhs = jnp.concatenate(lanes, axis=1)
                acc = acc + dot(lhs, c_ref[g, p * rank : p * rank + lhs.shape[1], :])
            blended.append(acc.astype(BF16))
        for g in range(regions):
            bl_ref[g, :, n * rank : (n + 1) * rank] = blended[g]
        if n < steps - 1:
            depth_k = 2 * rank * ((n + 2) // 2)
            at = first + n * held
            spot = (steps - 2 - n) * rank
            for g in range(regions):
                change = dot(bl_ref[g, :, :depth_k], qrev_ref[g, spot : spot + depth_k, :])
                keep(n, g, (rows_of(g, at, pulses).astype(F32) - change).astype(BF16))

    mine = place_ref[0]
    for n in range(steps):
        a_ref[n * pulses : (n + 1) * pulses, (steps - 1 - n) * rank :] = bl_ref[mine, :, : (n + 1) * rank]
    for b in range(blocks):
        response = jnp.concatenate([pays[k][b, pulses : pulses + rank, :] for k in reversed(range(steps))], axis=0)
        far = dot(a_ref[...], response)
        for n in range(steps):
            local = loc_ref[b] if n == steps - 1 else pays[n + 1][b, :pulses, :].astype(F32)
            out_ref[n, b] = (local - far[n * pulses : (n + 1) * pulses]).astype(BF16)


def on_device(
    incident,
    past_currents,
    self_inverse,
    near_tiles,
    near_cols,
    near_delay,
    block_slot,
    far_out,
    far_in,
    far_pairs,
    far_delay,
    far_coupling,
):
    steps, _, blocks, pulses, rows = incident.shape
    depth = past_currents.shape[0]
    near = near_cols.shape[2]
    farp, rank = far_coupling.shape[1:3]
    regions = lax.axis_size("region")
    ring = lax.axis_size("blk")
    device = lax.axis_index("blk")
    held = pulses + rank
    near_blocks = (2 * SPAN + 1) * 2 * blocks

    past, fin = past_currents[:, 0], far_in[0]

    first = held + (depth - 1) * pulses
    payload, moment, coupling = call(
        start_kernel,
        (
            shape((blocks, first, rows), BF16),
            shape((first, rank), F32),
            shape((4 * rank, 2 * rank), BF16),
        ),
        [in_hbm(x) for x in (past, fin, self_inverse[0], far_out[0], far_coupling[0], far_pairs, far_delay)],
        fetch=True,
    )
    fetched = [near_tiles[0], incident[:, 0], self_inverse[0], far_out[0]]
    code, offsets, tiles, inc, sinv, fout = pl.pallas_call(
        index_kernel,
        out_shape=(
            shape((blocks * near,), jnp.int32),
            shape((10,), jnp.int32),
            *(shape(x.shape, x.dtype) for x in fetched),
        ),
        in_specs=[pl.BlockSpec(memory_space=pltpu.SMEM)] * 4 + [pl.BlockSpec(memory_space=pltpu.HBM)] * 4,
        out_specs=(pl.BlockSpec(memory_space=pltpu.SMEM),) * 2 + (pl.BlockSpec(memory_space=pltpu.VMEM),) * 4,
        scratch_shapes=[pltpu.SemaphoreType.DMA((4,))],
        compiler_params=pltpu.CompilerParams(vmem_limit_bytes=VMEM_LIMIT),
        cost_estimate=pl.CostEstimate(flops=0, bytes_accessed=1 << 24, transcendentals=0),
    )(
        device.astype(jnp.int32).reshape(1),
        near_cols[0],
        near_delay[0],
        block_slot,
        *(in_hbm(x) for x in fetched),
    )
    pays, moms = [payload], [moment]
    hist = None
    hist_shape = shape((4 * near_blocks, held, rows), BF16)
    flops = 2 * blocks * near * held * rows * rows
    for n in range(steps):
        last = n == steps - 1
        packs = len(moms) if n == steps - 2 else 0
        pieces, code = window(payload, code) if n == 0 else (window(payload)[0], code)
        args = pieces + [in_vmem(tiles), inc, sinv, fout]
        aliases = {}
        if n > 0:
            args.append(in_vmem(hist))
            aliases = {2 + len(args) - 1: 1 if last else 0}
        loc_shape = shape((blocks, pulses, rows), F32)
        if last:
            outs = (loc_shape, hist_shape)
        elif packs:
            args += moms
            outs = (
                hist_shape,
                shape((blocks, held, rows), BF16),
                shape((512, 2 * rank), BF16),
                shape((blocks, pulses, rows), BF16),
            )
        else:
            outs = (hist_shape, shape((blocks, held, rows), BF16), shape((held, rank), F32))
        got = call(
            functools.partial(step_kernel, n, last, packs),
            outs,
            args,
            [code, offsets],
            aliases=aliases,
            flops=flops,
        )
        if last:
            loc = got[0]
        elif packs:
            hist, payload, packed, main = got
            pays.append(payload)
            payload = main
        else:
            hist, payload, moment = got
            pays.append(payload)
            moms.append(moment)

    packed, loc = lax.optimization_barrier((packed, loc))
    shares = lax.all_to_all(packed.reshape(ring, 512 // ring, 2 * rank), "blk", 0, 0, tiled=True)
    sums = call(sum_kernel, shape(shares.shape, BF16), [shares])
    sums = lax.all_to_all(sums, "blk", 0, 0, tiled=True).reshape(512, 2 * rank)
    place = jnp.stack([lax.axis_index("region"), device % 2]).astype(jnp.int32)
    halves = call(halves_kernel, shape((regions, 256 + 2 * rank, 2 * rank), BF16), [sums, coupling], [place])
    halves = lax.all_to_all(halves, "region", 0, 0, tiled=True)
    others = swap_cores(halves)

    currents = call(
        functools.partial(finish_kernel, steps, farp),
        shape((steps, blocks, pulses, rows), BF16),
        [halves, others, *pays, loc],
        [place],
        scratch=[
            pltpu.VMEM((regions, 512, 2 * rank), BF16),
            pltpu.VMEM((regions, 4 * rank, 2 * rank), BF16),
            pltpu.VMEM(((depth + steps) * regions, pulses, 2 * rank), BF16),
            pltpu.VMEM(((depth + steps) * regions, pulses, 2 * rank), BF16),
            pltpu.VMEM((regions, steps * rank, rank), BF16),
            pltpu.VMEM((regions, 8 * rank, rank), BF16),
            pltpu.VMEM((regions, pulses, steps * rank), BF16),
            pltpu.VMEM((steps * pulses, steps * rank), BF16),
            pltpu.VMEM((2 * regions, 128), jnp.int32),
            pltpu.SMEM((2 * regions, 128), jnp.int32),
            pltpu.SemaphoreType.DMA,
        ],
    )
    return currents[:, None]


def solution(mesh):
    in_specs = (
        P(None, "region", "blk", None, None),
        P(None, "region", "blk", None, None),
        P("region", "blk", None, None),
        P("region", "blk", None, None, None),
        P("region", "blk", None),
        P("region", "blk", None),
        P("region", None),
        P("region", "blk", None, None),
        P("region", "blk", None, None),
        P("region", None),
        P("region", None),
        P("region", None, None, None),
    )
    out_specs = P(None, "region", "blk", None, None)
    return jax.shard_map(on_device, mesh=mesh, in_specs=in_specs, out_specs=out_specs, check_vma=False)
```

```python
import functools

import jax
import jax.numpy as jnp
from jax import lax
from jax.experimental import pallas as pl
from jax.experimental.pallas import tpu as pltpu
from jax.sharding import PartitionSpec as P

SPAN = 2
TOGETHER = 4
VMEM_LIMIT = 12 * 2**20
F32 = jnp.float32
BF16 = jnp.bfloat16


def dot(a, b):
    return jnp.dot(a, b, preferred_element_type=F32)


def in_vmem(x):
    return pltpu.with_memory_space_constraint(x, pltpu.VMEM)


def in_hbm(x):
    return pltpu.with_memory_space_constraint(x, pltpu.HBM)


def call(kernel, out_shape, vmem_args, smem_args=(), scratch=(), aliases=None, flops=0, fetch=False):
    specs = [pl.BlockSpec(memory_space=pltpu.SMEM)] * len(smem_args)
    for arg in vmem_args:
        if fetch:
            specs.append(pl.BlockSpec(arg.shape, lambda i, n=arg.ndim: (0,) * n))
        else:
            specs.append(pl.BlockSpec(memory_space=pltpu.VMEM))
    return pl.pallas_call(
        kernel,
        grid=(1,) if fetch else (),
        out_shape=out_shape,
        in_specs=specs,
        out_specs=jax.tree.map(lambda _: pl.BlockSpec(memory_space=pltpu.VMEM), out_shape),
        scratch_shapes=list(scratch),
        input_output_aliases=aliases or {},
        compiler_params=pltpu.CompilerParams(vmem_limit_bytes=VMEM_LIMIT),
        cost_estimate=pl.CostEstimate(flops=flops, bytes_accessed=1 << 20, transcendentals=0),
    )(*smem_args, *vmem_args)


def shape(dims, dtype):
    return jax.ShapeDtypeStruct(dims, dtype)


def swap_cores(value):
    n = lax.axis_size("blk")
    return lax.ppermute(value, "blk", [(i, i ^ 1) for i in range(n)])


def paired(value, wanted, by):
    chips = lax.axis_size("blk") // 2
    pairs = []
    for c in range(chips - by):
        if wanted(c):
            for core in range(2):
                low, high = 2 * c + core, 2 * (c + by) + core
                pairs += [(low, high), (high, low)]
    return lax.ppermute(value, "blk", pairs)


def window(value, after=None):
    direct = [
        value,
        paired(value, lambda c: c % 2 == 0, 1),
        paired(value, lambda c: c % 4 < 2, 2),
        paired(value, lambda c: c % 2 == 1, 1),
        paired(value, lambda c: c % 4 >= 2, 2),
    ]
    if after is not None:
        direct[-1], after = lax.optimization_barrier((direct[-1], after))
    return direct + [swap_cores(v) for v in direct], after


def index_kernel(device_ref, cols_ref, delay_ref, slot_ref, *refs):
    count = (len(refs) - 4) // 2
    code_ref, off_ref, list_ref = refs[count : count + 3]
    sems = refs[-1]
    copies = [pltpu.make_async_copy(refs[i], refs[count + 3 + i], sems.at[i]) for i in range(count)]
    for copy in copies:
        copy.start()
    blocks, near = cols_ref.shape
    chip, core = device_ref[0] // 2, device_ref[0] % 2
    base = (chip - SPAN) * 2 * blocks
    top = (2 * SPAN + 1) * 2 * blocks - 1

    def row(b, spot):
        def one(j, spot):
            at = b * near + j
            local = jnp.clip(slot_ref[0, cols_ref[b, j]] - base, 0, top)
            delay = delay_ref[b, j]
            code_ref[at] = local * 8 + delay
            list_ref[spot] = at * 128 + local
            return spot + jnp.where(delay == 1, 1, 0)

        spot = lax.fori_loop(0, near, one, spot, unroll=8)
        list_ref[spot] = b * near * 128 + top + 1
        return spot + spot % 2

    spot = lax.fori_loop(0, blocks, row, 0)
    for i in range(2 * TOGETHER):
        list_ref[spot + i] = top + 1
    list_ref[list_ref.shape[0] - 1] = (spot + 2 * TOGETHER - 1) // (2 * TOGETHER)
    odd = jnp.where(chip % 2 == 0, 1, -1)
    two = jnp.where(chip % 4 < 2, 2, -2)
    for i, rel in enumerate((0, odd, two, -odd, -two)):
        off_ref[i] = ((rel + SPAN) * 2 + core) * blocks
        off_ref[i + 5] = ((rel + SPAN) * 2 + 1 - core) * blocks
    for copy in copies:
        copy.wait()


def start_kernel(past_ref, fin_ref, sinv_ref, fout_ref, coup_ref, pair_ref, delay_ref, pay_ref, mom_ref, send_ref):
    depth, blocks, pulses, _ = past_ref.shape
    rank = fin_ref.shape[1]
    farp = coup_ref.shape[0]
    for p in range(8):
        if p < farp:
            slab = coup_ref[p].astype(BF16)
        elif p == 7:
            row = lax.broadcasted_iota(jnp.int32, (rank, rank), 0)
            rest = jnp.zeros((1, rank - farp), jnp.int32)
            pair, delay = (jnp.concatenate([ref[...], rest], axis=1) for ref in (pair_ref, delay_ref))
            ints = jnp.where(row == 0, pair, jnp.where(row == 1, delay, 0))
            slab = ints.astype(F32).astype(BF16)
        else:
            slab = jnp.zeros((rank, rank), BF16)
        at, side = (p % 4) * rank, (p // 4) * rank
        send_ref[at : at + rank, side : side + rank] = slab
    total = jnp.zeros(mom_ref.shape, F32)
    for b in range(blocks):
        response = dot(fin_ref[b], sinv_ref[b]).astype(BF16)
        rows = [past_ref[0, b], response] + [past_ref[k, b] for k in range(1, depth)]
        whole = jnp.concatenate(rows, axis=0)
        pay_ref[b] = whole
        total = total + dot(whole, fout_ref[b])
    mom_ref[...] = total


def near_sum(step, b, rows, code_ref, tiles_ref, hist_ref, early=False):
    near = tiles_ref.shape[1]
    per_time = hist_ref.shape[0] // 4

    def source(at):
        code = code_ref[at]
        delay, local = code & 7, code >> 3
        if early:
            local = jnp.where(delay == 1, per_time - 1, local)
        return hist_ref[((step - delay) & 3) * per_time + local, :rows, :]

    acc = jnp.zeros((rows, tiles_ref.shape[3]), F32)
    for j in range(0, near, 2):
        at = b * near + j
        both = jnp.concatenate([source(at), source(at + 1)], axis=1)
        tile = tiles_ref[b, j : j + 2].reshape(-1, tiles_ref.shape[3])
        acc = acc + dot(both, tile)
    return acc


def early_kernel(step, code_ref, tiles_ref, hist_ref, acc_ref):
    def row(b, _):
        acc_ref[b] = near_sum(step, b, acc_ref.shape[1], code_ref, tiles_ref, hist_ref, early=True)
        return 0

    lax.fori_loop(0, acc_ref.shape[0], row, 0)


def step_kernel(step, last, packs, *refs):
    refs = list(refs)
    code_ref, off_ref, list_ref = refs[:3]
    pieces = refs[3:13]
    tiles_ref, inc_ref, sinv_ref, fout_ref = refs[13:17]
    rest = refs[17:]
    moms = []
    if step > 0:
        early_ref, sum_ref = rest[1], rest[-1]
        rest = rest[2:-1]
    if packs:
        moms, rest = rest[:packs], rest[packs:]
    blocks, near = tiles_ref.shape[:2]
    pulses = inc_ref.shape[2]
    if last:
        loc_ref, hist_ref = rest
        rows = pulses
    else:
        hist_ref, pay_ref, mom_ref = rest[:3]
        rows = pay_ref.shape[1]
    per_time = hist_ref.shape[0] // 4
    held = hist_ref.shape[1]

    if step == 0:
        for k in range(1, 4):
            hist_ref[pl.ds((3 - k) * per_time, per_time), pulses:held, :] = jnp.zeros(
                (per_time, held - pulses, hist_ref.shape[2]), BF16
            )
        for k in range(4):
            hist_ref[(k + 1) * per_time - 1] = jnp.zeros(hist_ref.shape[1:], BF16)
    for i, piece in enumerate(pieces):
        off = off_ref[i]
        if step == 0:
            hist_ref[pl.ds(3 * per_time + off, blocks), :, :] = piece[:, :held, :]
            for k in range(1, 4):
                row = held + (k - 1) * pulses
                hist_ref[pl.ds((3 - k) * per_time + off, blocks), :pulses, :] = piece[:, row : row + pulses, :]
        else:
            hist_ref[pl.ds(((step - 1) % 4) * per_time + off, blocks), :rows, :] = piece[...]

    if step > 0:
        newest = ((step - 1) & 3) * per_time
        sum_ref[...] = early_ref[...]

        def turn(i, _):
            sums = []
            for pair in range(TOGETHER):
                one, two = (list_ref[(i * TOGETHER + pair) * 2 + k] for k in range(2))
                both = jnp.concatenate([hist_ref[newest + (c & 127), :rows, :] for c in (one, two)], axis=1)
                at = [c >> 7 for c in (one, two)]
                tile = jnp.concatenate([tiles_ref[t // near, t % near] for t in at], axis=0)
                sums.append((at[0] // near, dot(both, tile)))
            for b, value in sums:
                sum_ref[b] += value
            return 0

        lax.fori_loop(0, list_ref[list_ref.shape[0] - 1], turn, 0)

    def row(b, total):
        if step == 0:
            acc = near_sum(step, b, rows, code_ref, tiles_ref, hist_ref)
        else:
            acc = sum_ref[b]
        main = inc_ref[step, b].astype(F32) - acc[:pulses]
        driven = main if last else jnp.concatenate([main, -acc[pulses:]], axis=0)
        current = dot(driven.astype(BF16), sinv_ref[b])
        if last:
            loc_ref[b] = current
            return total
        rounded = current.astype(BF16)
        pay_ref[b] = rounded
        return total + dot(rounded, fout_ref[b])

    start = jnp.zeros((rows, fout_ref.shape[2]), F32)
    total = lax.fori_loop(0, blocks, row, start, unroll=step > 0)
    if last:
        return
    if not packs:
        mom_ref[...] = total
        return
    main_ref = rest[3]
    main_ref[...] = pay_ref[:, :pulses, :]
    listed = [m[...] for m in moms] + [total[:pulses]]
    every = jnp.concatenate(listed, axis=0).astype(BF16)
    half, rank = every.shape[0] // 2, every.shape[1]
    mom_ref[:half, :rank] = every[:half]
    mom_ref[:half, rank:] = every[half:]
    mom_ref[half:, :] = jnp.zeros((mom_ref.shape[0] - half, mom_ref.shape[1]), BF16)


def sum_kernel(in_ref, out_ref):
    total = in_ref[0].astype(F32)
    for i in range(1, in_ref.shape[0]):
        total = total + in_ref[i].astype(F32)
    for i in range(out_ref.shape[0]):
        out_ref[i] = total.astype(BF16)


def halves_kernel(place_ref, sums_ref, coup_ref, out_ref):
    core = place_ref[1]
    for i, ref in ((0, sums_ref), (sums_ref.shape[0] // 2, coup_ref)):
        rows = ref.shape[0] // 2
        half = ref[pl.ds(pl.multiple_of(core * rows, rows), rows), :]
        for g in range(out_ref.shape[0]):
            out_ref[g, i : i + rows, :] = half


def finish_kernel(steps, farp, place_ref, mine_ref, other_ref, *refs):
    pays = refs[:steps]
    loc_ref, out_ref, got_ref, coup_ref, low_ref, high_ref, qrev_ref, c_ref, bl_ref, a_ref, ints_ref, num_ref, sem = refs[steps:]
    regions = got_ref.shape[0]
    depth = 4
    blocks, pulses = loc_ref.shape[:2]
    rank = coup_ref.shape[2] // 2
    held = pulses + rank
    first = held + (depth - 1) * pulses
    half = (first + (steps - 2) * held + pulses) // 2

    for ref, core in ((mine_ref, place_ref[1]), (other_ref, 1 - place_ref[1])):
        for whole, at in ((got_ref, 0), (coup_ref, got_ref.shape[1] // 2)):
            rows = whole.shape[1] // 2
            whole[:, pl.ds(pl.multiple_of(core * rows, rows), rows), :] = ref[:, at : at + rows, :]

    ints_ref[...] = jnp.zeros(ints_ref.shape, jnp.int32)
    for g in range(regions):
        numbers = coup_ref[g, 3 * rank : 3 * rank + 16, rank:].astype(F32).astype(jnp.int32)
        ints_ref[2 * g : 2 * g + 2, :rank] = numbers[:2]
    copy = pltpu.make_async_copy(ints_ref, num_ref, sem)
    copy.start()

    def rows_of(g, at, count):
        parts = []
        for r in range(at, at + count, 16):
            side, row = divmod(r, half)
            parts.append(got_ref[g, row : row + 16, side * rank : (side + 1) * rank])
        return jnp.concatenate(parts, axis=0)

    def keep(time, g, value):
        low_ref[(time + depth) * regions + g, :, :rank] = value
        high_ref[(time + depth) * regions + g, :, rank:] = value

    def source(n, g, q):
        return (n - num_ref[2 * g + 1, q] + depth) * regions + num_ref[2 * g, q]

    low_ref[...] = jnp.zeros(low_ref.shape, BF16)
    high_ref[...] = jnp.zeros(high_ref.shape, BF16)
    bl_ref[...] = jnp.zeros(bl_ref.shape, BF16)
    a_ref[...] = jnp.zeros(a_ref.shape, BF16)
    for g in range(regions):
        keep(-1, g, rows_of(g, 0, pulses))
        for k in range(1, depth):
            keep(-1 - k, g, rows_of(g, held + (k - 1) * pulses, pulses))
        for lag in range(steps - 1):
            at = pulses if lag == 0 else first + (lag - 1) * held + pulses
            spot = (steps - 2 - lag) * rank
            qrev_ref[g, spot : spot + rank, :] = rows_of(g, at, rank)
        qrev_ref[g, (steps - 1) * rank :, :] = jnp.zeros((rank, rank), BF16)
        for p in range(8):
            c_ref[g, p * rank : (p + 1) * rank, :] = (
                coup_ref[g, (p % 4) * rank : (p % 4 + 1) * rank, (p // 4) * rank : (p // 4 + 1) * rank]
                if p < farp
                else jnp.zeros((rank, rank), BF16)
            )

    copy.wait()
    for n in range(steps):
        blended = []
        for g in range(regions):
            acc = jnp.zeros((pulses, rank), F32)
            for p in range(0, farp, 4):
                lanes = []
                for q in range(p, min(p + 4, farp), 2):
                    part = low_ref[source(n, g, q)]
                    if q + 1 < farp:
                        part = part + high_ref[source(n, g, q + 1)]
                    lanes.append(part)
                lhs = jnp.concatenate(lanes, axis=1)
                acc = acc + dot(lhs, c_ref[g, p * rank : p * rank + lhs.shape[1], :])
            blended.append(acc.astype(BF16))
        for g in range(regions):
            bl_ref[g, :, n * rank : (n + 1) * rank] = blended[g]
        if n < steps - 1:
            depth_k = 2 * rank * ((n + 2) // 2)
            at = first + n * held
            spot = (steps - 2 - n) * rank
            for g in range(regions):
                change = dot(bl_ref[g, :, :depth_k], qrev_ref[g, spot : spot + depth_k, :])
                keep(n, g, (rows_of(g, at, pulses).astype(F32) - change).astype(BF16))

    mine = place_ref[0]
    for n in range(steps):
        a_ref[n * pulses : (n + 1) * pulses, (steps - 1 - n) * rank :] = bl_ref[mine, :, : (n + 1) * rank]
    for b in range(blocks):
        response = jnp.concatenate([pays[k][b, pulses : pulses + rank, :] for k in reversed(range(steps))], axis=0)
        far = dot(a_ref[...], response)
        for n in range(steps):
            local = loc_ref[b] if n == steps - 1 else pays[n + 1][b, :pulses, :].astype(F32)
            out_ref[n, b] = (local - far[n * pulses : (n + 1) * pulses]).astype(BF16)


def on_device(
    incident,
    past_currents,
    self_inverse,
    near_tiles,
    near_cols,
    near_delay,
    block_slot,
    far_out,
    far_in,
    far_pairs,
    far_delay,
    far_coupling,
):
    steps, _, blocks, pulses, rows = incident.shape
    depth = past_currents.shape[0]
    near = near_cols.shape[2]
    farp, rank = far_coupling.shape[1:3]
    regions = lax.axis_size("region")
    ring = lax.axis_size("blk")
    device = lax.axis_index("blk")
    held = pulses + rank
    near_blocks = (2 * SPAN + 1) * 2 * blocks + 1

    past, fin = past_currents[:, 0], far_in[0]

    first = held + (depth - 1) * pulses
    payload, moment, coupling = call(
        start_kernel,
        (
            shape((blocks, first, rows), BF16),
            shape((first, rank), F32),
            shape((4 * rank, 2 * rank), BF16),
        ),
        [in_hbm(x) for x in (past, fin, self_inverse[0], far_out[0], far_coupling[0], far_pairs, far_delay)],
        fetch=True,
    )
    fetched = [near_tiles[0], incident[:, 0], self_inverse[0], far_out[0]]
    code, offsets, late, tiles, inc, sinv, fout = pl.pallas_call(
        index_kernel,
        out_shape=(
            shape((blocks * near,), jnp.int32),
            shape((10,), jnp.int32),
            shape((blocks * (near + 1) + 2 * TOGETHER + 8,), jnp.int32),
            *(shape(x.shape, x.dtype) for x in fetched),
        ),
        in_specs=[pl.BlockSpec(memory_space=pltpu.SMEM)] * 4 + [pl.BlockSpec(memory_space=pltpu.HBM)] * 4,
        out_specs=(pl.BlockSpec(memory_space=pltpu.SMEM),) * 3 + (pl.BlockSpec(memory_space=pltpu.VMEM),) * 4,
        scratch_shapes=[pltpu.SemaphoreType.DMA((4,))],
        compiler_params=pltpu.CompilerParams(vmem_limit_bytes=VMEM_LIMIT),
        cost_estimate=pl.CostEstimate(flops=0, bytes_accessed=1 << 24, transcendentals=0),
    )(
        device.astype(jnp.int32).reshape(1),
        near_cols[0],
        near_delay[0],
        block_slot,
        *(in_hbm(x) for x in fetched),
    )
    pays, moms = [payload], [moment]
    hist = None
    hist_shape = shape((4 * near_blocks, held, rows), BF16)
    flops = 2 * blocks * near * held * rows * rows
    for n in range(steps):
        last = n == steps - 1
        packs = len(moms) if n == steps - 2 else 0
        tail, aliases, scratch = [], {}, []
        if n == 0:
            pieces, code = window(payload, code)
        else:
            wide = pulses if last else held
            early = call(
                functools.partial(early_kernel, n),
                shape((blocks, wide, rows), F32),
                [in_vmem(tiles), in_vmem(hist)],
                [code],
                flops=flops,
            )
            pieces, early = window(payload, early)
            tail = [in_vmem(hist), early]
            scratch = [pltpu.VMEM((blocks, wide, rows), F32)]
        args = pieces + [in_vmem(tiles), inc, sinv, fout] + tail
        if n > 0:
            aliases = {3 + len(args) - 2: 1 if last else 0}
        loc_shape = shape((blocks, pulses, rows), F32)
        if last:
            outs = (loc_shape, hist_shape)
        elif packs:
            args += moms
            outs = (
                hist_shape,
                shape((blocks, held, rows), BF16),
                shape((512, 2 * rank), BF16),
                shape((blocks, pulses, rows), BF16),
            )
        else:
            outs = (hist_shape, shape((blocks, held, rows), BF16), shape((held, rank), F32))
        got = call(
            functools.partial(step_kernel, n, last, packs),
            outs,
            args,
            [code, offsets, late],
            scratch=scratch,
            aliases=aliases,
            flops=flops,
        )
        if last:
            loc = got[0]
        elif packs:
            hist, payload, packed, main = got
            pays.append(payload)
            payload = main
        else:
            hist, payload, moment = got
            pays.append(payload)
            moms.append(moment)

    packed, loc = lax.optimization_barrier((packed, loc))
    shares = lax.all_to_all(packed.reshape(ring, 512 // ring, 2 * rank), "blk", 0, 0, tiled=True)
    sums = call(sum_kernel, shape(shares.shape, BF16), [shares])
    sums = lax.all_to_all(sums, "blk", 0, 0, tiled=True).reshape(512, 2 * rank)
    place = jnp.stack([lax.axis_index("region"), device % 2]).astype(jnp.int32)
    halves = call(halves_kernel, shape((regions, 256 + 2 * rank, 2 * rank), BF16), [sums, coupling], [place])
    halves = lax.all_to_all(halves, "region", 0, 0, tiled=True)
    others = swap_cores(halves)

    currents = call(
        functools.partial(finish_kernel, steps, farp),
        shape((steps, blocks, pulses, rows), BF16),
        [halves, others, *pays, loc],
        [place],
        scratch=[
            pltpu.VMEM((regions, 512, 2 * rank), BF16),
            pltpu.VMEM((regions, 4 * rank, 2 * rank), BF16),
            pltpu.VMEM(((depth + steps) * regions, pulses, 2 * rank), BF16),
            pltpu.VMEM(((depth + steps) * regions, pulses, 2 * rank), BF16),
            pltpu.VMEM((regions, steps * rank, rank), BF16),
            pltpu.VMEM((regions, 8 * rank, rank), BF16),
            pltpu.VMEM((regions, pulses, steps * rank), BF16),
            pltpu.VMEM((steps * pulses, steps * rank), BF16),
            pltpu.VMEM((2 * regions, 128), jnp.int32),
            pltpu.SMEM((2 * regions, 128), jnp.int32),
            pltpu.SemaphoreType.DMA,
        ],
    )
    return currents[:, None]


def solution(mesh):
    in_specs = (
        P(None, "region", "blk", None, None),
        P(None, "region", "blk", None, None),
        P("region", "blk", None, None),
        P("region", "blk", None, None, None),
        P("region", "blk", None),
        P("region", "blk", None),
        P("region", None),
        P("region", "blk", None, None),
        P("region", "blk", None, None),
        P("region", None),
        P("region", None),
        P("region", None, None, None),
    )
    out_specs = P(None, "region", "blk", None, None)
    return jax.shard_map(on_device, mesh=mesh, in_specs=in_specs, out_specs=out_specs, check_vma=False)
```

```python
import functools

import jax
import jax.numpy as jnp
from jax import lax
from jax.experimental import pallas as pl
from jax.experimental.pallas import tpu as pltpu
from jax.sharding import PartitionSpec as P

SPAN = 2
TOGETHER = 4
VMEM_LIMIT = 12 * 2**20
F32 = jnp.float32
BF16 = jnp.bfloat16


def dot(a, b):
    return jnp.dot(a, b, preferred_element_type=F32)


def in_vmem(x):
    return pltpu.with_memory_space_constraint(x, pltpu.VMEM)


def in_hbm(x):
    return pltpu.with_memory_space_constraint(x, pltpu.HBM)


def call(kernel, out_shape, vmem_args, smem_args=(), scratch=(), aliases=None, flops=0, fetch=False):
    specs = [pl.BlockSpec(memory_space=pltpu.SMEM)] * len(smem_args)
    for arg in vmem_args:
        if fetch:
            specs.append(pl.BlockSpec(arg.shape, lambda i, n=arg.ndim: (0,) * n))
        else:
            specs.append(pl.BlockSpec(memory_space=pltpu.VMEM))
    return pl.pallas_call(
        kernel,
        grid=(1,) if fetch else (),
        out_shape=out_shape,
        in_specs=specs,
        out_specs=jax.tree.map(lambda _: pl.BlockSpec(memory_space=pltpu.VMEM), out_shape),
        scratch_shapes=list(scratch),
        input_output_aliases=aliases or {},
        compiler_params=pltpu.CompilerParams(vmem_limit_bytes=VMEM_LIMIT),
        cost_estimate=pl.CostEstimate(flops=flops, bytes_accessed=1 << 20, transcendentals=0),
    )(*smem_args, *vmem_args)


def shape(dims, dtype):
    return jax.ShapeDtypeStruct(dims, dtype)


def swap_cores(value):
    n = lax.axis_size("blk")
    return lax.ppermute(value, "blk", [(i, i ^ 1) for i in range(n)])


def paired(value, wanted, by):
    chips = lax.axis_size("blk") // 2
    pairs = []
    for c in range(chips - by):
        if wanted(c):
            for core in range(2):
                low, high = 2 * c + core, 2 * (c + by) + core
                pairs += [(low, high), (high, low)]
    return lax.ppermute(value, "blk", pairs)


def even_pairs(value):
    return paired(value, lambda c: c % 2 == 0, 1)


def odd_pairs(value):
    return paired(value, lambda c: c % 2 == 1, 1)


def window(value, beside):
    other = odd_pairs(value)
    near = even_pairs(value)
    other, made = beside(other)
    passed = odd_pairs(near)
    last = even_pairs(other)
    last, made = lax.optimization_barrier((last, made))
    direct = [value, near, other, last, passed]
    return direct + [swap_cores(v) for v in direct], made


def index_kernel(device_ref, cols_ref, delay_ref, slot_ref, *refs):
    count = (len(refs) - 4) // 2
    code_ref, off_ref, list_ref = refs[count : count + 3]
    sems = refs[-1]
    copies = [pltpu.make_async_copy(refs[i], refs[count + 3 + i], sems.at[i]) for i in range(count)]
    for copy in copies:
        copy.start()
    blocks, near = cols_ref.shape
    chip, core = device_ref[0] // 2, device_ref[0] % 2
    base = (chip - SPAN) * 2 * blocks
    top = (2 * SPAN + 1) * 2 * blocks - 1

    def row(b, spot):
        def one(j, spot):
            at = b * near + j
            local = jnp.clip(slot_ref[0, cols_ref[b, j]] - base, 0, top)
            delay = delay_ref[b, j]
            code_ref[at] = local * 8 + delay
            list_ref[spot] = at * 128 + local
            return spot + jnp.where(delay == 1, 1, 0)

        spot = lax.fori_loop(0, near, one, spot, unroll=8)
        list_ref[spot] = b * near * 128 + top + 1
        return spot + spot % 2

    spot = lax.fori_loop(0, blocks, row, 0)
    for i in range(2 * TOGETHER):
        list_ref[spot + i] = top + 1
    list_ref[list_ref.shape[0] - 1] = (spot + 2 * TOGETHER - 1) // (2 * TOGETHER)
    odd = jnp.where(chip % 2 == 0, 1, -1)
    for i, rel in enumerate((0, odd, -odd, 2 * odd, -2 * odd)):
        off_ref[i] = ((rel + SPAN) * 2 + core) * blocks
        off_ref[i + 5] = ((rel + SPAN) * 2 + 1 - core) * blocks
    for copy in copies:
        copy.wait()


def start_kernel(past_ref, fin_ref, sinv_ref, fout_ref, coup_ref, pair_ref, delay_ref, pay_ref, mom_ref, send_ref):
    depth, blocks, pulses, _ = past_ref.shape
    rank = fin_ref.shape[1]
    farp = coup_ref.shape[0]
    for p in range(8):
        if p < farp:
            slab = coup_ref[p].astype(BF16)
        elif p == 7:
            row = lax.broadcasted_iota(jnp.int32, (rank, rank), 0)
            rest = jnp.zeros((1, rank - farp), jnp.int32)
            pair, delay = (jnp.concatenate([ref[...], rest], axis=1) for ref in (pair_ref, delay_ref))
            ints = jnp.where(row == 0, pair, jnp.where(row == 1, delay, 0))
            slab = ints.astype(F32).astype(BF16)
        else:
            slab = jnp.zeros((rank, rank), BF16)
        at, side = (p % 4) * rank, (p // 4) * rank
        send_ref[at : at + rank, side : side + rank] = slab
    total = jnp.zeros(mom_ref.shape, F32)
    for b in range(blocks):
        response = dot(fin_ref[b], sinv_ref[b]).astype(BF16)
        rows = [past_ref[0, b], response] + [past_ref[k, b] for k in range(1, depth)]
        whole = jnp.concatenate(rows, axis=0)
        pay_ref[b] = whole
        total = total + dot(whole, fout_ref[b])
    mom_ref[...] = total


def near_sum(step, b, rows, code_ref, tiles_ref, hist_ref, early=False):
    near = tiles_ref.shape[1]
    per_time = hist_ref.shape[0] // 4

    def source(at):
        code = code_ref[at]
        delay, local = code & 7, code >> 3
        if early:
            local = jnp.where(delay == 1, per_time - 1, local)
        return hist_ref[((step - delay) & 3) * per_time + local, :rows, :]

    acc = jnp.zeros((rows, tiles_ref.shape[3]), F32)
    for j in range(0, near, 2):
        at = b * near + j
        both = jnp.concatenate([source(at), source(at + 1)], axis=1)
        tile = tiles_ref[b, j : j + 2].reshape(-1, tiles_ref.shape[3])
        acc = acc + dot(both, tile)
    return acc


def early_kernel(step, code_ref, tiles_ref, hist_ref, acc_ref):
    def row(b, _):
        acc_ref[b] = near_sum(step, b, acc_ref.shape[1], code_ref, tiles_ref, hist_ref, early=True)
        return 0

    lax.fori_loop(0, acc_ref.shape[0], row, 0)


def step_kernel(step, last, packs, *refs):
    refs = list(refs)
    code_ref, off_ref, list_ref = refs[:3]
    pieces = refs[3:13]
    tiles_ref, inc_ref, sinv_ref, fout_ref = refs[13:17]
    rest = refs[17:]
    moms = []
    if step > 0:
        early_ref, sum_ref = rest[1], rest[-1]
        rest = rest[2:-1]
    if packs:
        moms, rest = rest[:packs], rest[packs:]
    blocks, near = tiles_ref.shape[:2]
    pulses = inc_ref.shape[2]
    if last:
        loc_ref, hist_ref = rest
        rows = pulses
    else:
        hist_ref, pay_ref, mom_ref = rest[:3]
        rows = pay_ref.shape[1]
    per_time = hist_ref.shape[0] // 4
    held = hist_ref.shape[1]

    if step == 0:
        for k in range(1, 4):
            hist_ref[pl.ds((3 - k) * per_time, per_time), pulses:held, :] = jnp.zeros(
                (per_time, held - pulses, hist_ref.shape[2]), BF16
            )
        for k in range(4):
            hist_ref[(k + 1) * per_time - 1] = jnp.zeros(hist_ref.shape[1:], BF16)
    for i, piece in enumerate(pieces):
        off = off_ref[i]
        if step == 0:
            hist_ref[pl.ds(3 * per_time + off, blocks), :, :] = piece[:, :held, :]
            for k in range(1, 4):
                row = held + (k - 1) * pulses
                hist_ref[pl.ds((3 - k) * per_time + off, blocks), :pulses, :] = piece[:, row : row + pulses, :]
        else:
            hist_ref[pl.ds(((step - 1) % 4) * per_time + off, blocks), :rows, :] = piece[...]

    if step > 0:
        newest = ((step - 1) & 3) * per_time
        sum_ref[...] = early_ref[...]

        def turn(i, _):
            sums = []
            for pair in range(TOGETHER):
                one, two = (list_ref[(i * TOGETHER + pair) * 2 + k] for k in range(2))
                both = jnp.concatenate([hist_ref[newest + (c & 127), :rows, :] for c in (one, two)], axis=1)
                at = [c >> 7 for c in (one, two)]
                tile = jnp.concatenate([tiles_ref[t // near, t % near] for t in at], axis=0)
                sums.append((at[0] // near, dot(both, tile)))
            for b, value in sums:
                sum_ref[b] += value
            return 0

        lax.fori_loop(0, list_ref[list_ref.shape[0] - 1], turn, 0)

    def row(b, total):
        if step == 0:
            acc = near_sum(step, b, rows, code_ref, tiles_ref, hist_ref)
        else:
            acc = sum_ref[b]
        main = inc_ref[step, b].astype(F32) - acc[:pulses]
        driven = main if last else jnp.concatenate([main, -acc[pulses:]], axis=0)
        current = dot(driven.astype(BF16), sinv_ref[b])
        if last:
            loc_ref[b] = current
            return total
        rounded = current.astype(BF16)
        pay_ref[b] = rounded
        return total + dot(rounded, fout_ref[b])

    start = jnp.zeros((rows, fout_ref.shape[2]), F32)
    total = lax.fori_loop(0, blocks, row, start, unroll=step > 0)
    if last:
        return
    if not packs:
        mom_ref[...] = total
        return
    main_ref = rest[3]
    main_ref[...] = pay_ref[:, :pulses, :]
    listed = [m[...] for m in moms] + [total[:pulses]]
    every = jnp.concatenate(listed, axis=0).astype(BF16)
    half, rank = every.shape[0] // 2, every.shape[1]
    mom_ref[:half, :rank] = every[:half]
    mom_ref[:half, rank:] = every[half:]
    mom_ref[half:, :] = jnp.zeros((mom_ref.shape[0] - half, mom_ref.shape[1]), BF16)


def sum_kernel(in_ref, out_ref):
    total = in_ref[0].astype(F32)
    for i in range(1, in_ref.shape[0]):
        total = total + in_ref[i].astype(F32)
    for i in range(out_ref.shape[0]):
        out_ref[i] = total.astype(BF16)


def halves_kernel(place_ref, sums_ref, coup_ref, out_ref):
    core = place_ref[1]
    for i, ref in ((0, sums_ref), (sums_ref.shape[0] // 2, coup_ref)):
        rows = ref.shape[0] // 2
        half = ref[pl.ds(pl.multiple_of(core * rows, rows), rows), :]
        for g in range(out_ref.shape[0]):
            out_ref[g, i : i + rows, :] = half


def finish_kernel(steps, farp, place_ref, mine_ref, other_ref, *refs):
    pays = refs[:steps]
    loc_ref, out_ref, got_ref, coup_ref, low_ref, high_ref, qrev_ref, c_ref, bl_ref, a_ref, ints_ref, num_ref, sem = refs[steps:]
    regions = got_ref.shape[0]
    depth = 4
    blocks, pulses = loc_ref.shape[:2]
    rank = coup_ref.shape[2] // 2
    held = pulses + rank
    first = held + (depth - 1) * pulses
    half = (first + (steps - 2) * held + pulses) // 2

    for ref, core in ((mine_ref, place_ref[1]), (other_ref, 1 - place_ref[1])):
        for whole, at in ((got_ref, 0), (coup_ref, got_ref.shape[1] // 2)):
            rows = whole.shape[1] // 2
            whole[:, pl.ds(pl.multiple_of(core * rows, rows), rows), :] = ref[:, at : at + rows, :]

    ints_ref[...] = jnp.zeros(ints_ref.shape, jnp.int32)
    for g in range(regions):
        numbers = coup_ref[g, 3 * rank : 3 * rank + 16, rank:].astype(F32).astype(jnp.int32)
        ints_ref[2 * g : 2 * g + 2, :rank] = numbers[:2]
    copy = pltpu.make_async_copy(ints_ref, num_ref, sem)
    copy.start()

    def rows_of(g, at, count):
        parts = []
        for r in range(at, at + count, 16):
            side, row = divmod(r, half)
            parts.append(got_ref[g, row : row + 16, side * rank : (side + 1) * rank])
        return jnp.concatenate(parts, axis=0)

    def keep(time, g, value):
        low_ref[(time + depth) * regions + g, :, :rank] = value
        high_ref[(time + depth) * regions + g, :, rank:] = value

    def source(n, g, q):
        return (n - num_ref[2 * g + 1, q] + depth) * regions + num_ref[2 * g, q]

    low_ref[...] = jnp.zeros(low_ref.shape, BF16)
    high_ref[...] = jnp.zeros(high_ref.shape, BF16)
    bl_ref[...] = jnp.zeros(bl_ref.shape, BF16)
    a_ref[...] = jnp.zeros(a_ref.shape, BF16)
    for g in range(regions):
        keep(-1, g, rows_of(g, 0, pulses))
        for k in range(1, depth):
            keep(-1 - k, g, rows_of(g, held + (k - 1) * pulses, pulses))
        for lag in range(steps - 1):
            at = pulses if lag == 0 else first + (lag - 1) * held + pulses
            spot = (steps - 2 - lag) * rank
            qrev_ref[g, spot : spot + rank, :] = rows_of(g, at, rank)
        qrev_ref[g, (steps - 1) * rank :, :] = jnp.zeros((rank, rank), BF16)
        for p in range(8):
            c_ref[g, p * rank : (p + 1) * rank, :] = (
                coup_ref[g, (p % 4) * rank : (p % 4 + 1) * rank, (p // 4) * rank : (p // 4 + 1) * rank]
                if p < farp
                else jnp.zeros((rank, rank), BF16)
            )

    copy.wait()
    for n in range(steps):
        blended = []
        for g in range(regions):
            acc = jnp.zeros((pulses, rank), F32)
            for p in range(0, farp, 4):
                lanes = []
                for q in range(p, min(p + 4, farp), 2):
                    part = low_ref[source(n, g, q)]
                    if q + 1 < farp:
                        part = part + high_ref[source(n, g, q + 1)]
                    lanes.append(part)
                lhs = jnp.concatenate(lanes, axis=1)
                acc = acc + dot(lhs, c_ref[g, p * rank : p * rank + lhs.shape[1], :])
            blended.append(acc.astype(BF16))
        for g in range(regions):
            bl_ref[g, :, n * rank : (n + 1) * rank] = blended[g]
        if n < steps - 1:
            depth_k = 2 * rank * ((n + 2) // 2)
            at = first + n * held
            spot = (steps - 2 - n) * rank
            for g in range(regions):
                change = dot(bl_ref[g, :, :depth_k], qrev_ref[g, spot : spot + depth_k, :])
                keep(n, g, (rows_of(g, at, pulses).astype(F32) - change).astype(BF16))

    mine = place_ref[0]
    for n in range(steps):
        a_ref[n * pulses : (n + 1) * pulses, (steps - 1 - n) * rank :] = bl_ref[mine, :, : (n + 1) * rank]
    for b in range(blocks):
        response = jnp.concatenate([pays[k][b, pulses : pulses + rank, :] for k in reversed(range(steps))], axis=0)
        far = dot(a_ref[...], response)
        for n in range(steps):
            local = loc_ref[b] if n == steps - 1 else pays[n + 1][b, :pulses, :].astype(F32)
            out_ref[n, b] = (local - far[n * pulses : (n + 1) * pulses]).astype(BF16)


def on_device(
    incident,
    past_currents,
    self_inverse,
    near_tiles,
    near_cols,
    near_delay,
    block_slot,
    far_out,
    far_in,
    far_pairs,
    far_delay,
    far_coupling,
):
    steps, _, blocks, pulses, rows = incident.shape
    depth = past_currents.shape[0]
    near = near_cols.shape[2]
    farp, rank = far_coupling.shape[1:3]
    regions = lax.axis_size("region")
    ring = lax.axis_size("blk")
    device = lax.axis_index("blk")
    held = pulses + rank
    near_blocks = (2 * SPAN + 1) * 2 * blocks + 1

    past, fin = past_currents[:, 0], far_in[0]

    first = held + (depth - 1) * pulses
    payload, moment, coupling = call(
        start_kernel,
        (
            shape((blocks, first, rows), BF16),
            shape((first, rank), F32),
            shape((4 * rank, 2 * rank), BF16),
        ),
        [in_hbm(x) for x in (past, fin, self_inverse[0], far_out[0], far_coupling[0], far_pairs, far_delay)],
        fetch=True,
    )
    fetched = [near_tiles[0], incident[:, 0], self_inverse[0], far_out[0]]
    code, offsets, late, tiles, inc, sinv, fout = pl.pallas_call(
        index_kernel,
        out_shape=(
            shape((blocks * near,), jnp.int32),
            shape((10,), jnp.int32),
            shape((blocks * (near + 1) + 2 * TOGETHER + 8,), jnp.int32),
            *(shape(x.shape, x.dtype) for x in fetched),
        ),
        in_specs=[pl.BlockSpec(memory_space=pltpu.SMEM)] * 4 + [pl.BlockSpec(memory_space=pltpu.HBM)] * 4,
        out_specs=(pl.BlockSpec(memory_space=pltpu.SMEM),) * 3 + (pl.BlockSpec(memory_space=pltpu.VMEM),) * 4,
        scratch_shapes=[pltpu.SemaphoreType.DMA((4,))],
        compiler_params=pltpu.CompilerParams(vmem_limit_bytes=VMEM_LIMIT),
        cost_estimate=pl.CostEstimate(flops=0, bytes_accessed=1 << 24, transcendentals=0),
    )(
        device.astype(jnp.int32).reshape(1),
        near_cols[0],
        near_delay[0],
        block_slot,
        *(in_hbm(x) for x in fetched),
    )
    pays, moms = [payload], [moment]
    hist = None
    hist_shape = shape((4 * near_blocks, held, rows), BF16)
    flops = 2 * blocks * near * held * rows * rows
    for n in range(steps):
        last = n == steps - 1
        packs = len(moms) if n == steps - 2 else 0
        tail, aliases, scratch = [], {}, []
        if n == 0:
            pieces, code = window(payload, lambda arrived: (arrived, code))
        else:
            wide = pulses if last else held

            def beside(arrived):
                arrived, codes = lax.optimization_barrier((arrived, code))
                early = call(
                    functools.partial(early_kernel, n),
                    shape((blocks, wide, rows), F32),
                    [in_vmem(tiles), in_vmem(hist)],
                    [codes],
                    flops=flops,
                )
                return arrived, early

            pieces, early = window(payload, beside)
            tail = [in_vmem(hist), early]
            scratch = [pltpu.VMEM((blocks, wide, rows), F32)]
        args = pieces + [in_vmem(tiles), inc, sinv, fout] + tail
        if n > 0:
            aliases = {3 + len(args) - 2: 1 if last else 0}
        loc_shape = shape((blocks, pulses, rows), F32)
        if last:
            outs = (loc_shape, hist_shape)
        elif packs:
            args += moms
            outs = (
                hist_shape,
                shape((blocks, held, rows), BF16),
                shape((512, 2 * rank), BF16),
                shape((blocks, pulses, rows), BF16),
            )
        else:
            outs = (hist_shape, shape((blocks, held, rows), BF16), shape((held, rank), F32))
        got = call(
            functools.partial(step_kernel, n, last, packs),
            outs,
            args,
            [code, offsets, late],
            scratch=scratch,
            aliases=aliases,
            flops=flops,
        )
        if last:
            loc = got[0]
        elif packs:
            hist, payload, packed, main = got
            pays.append(payload)
            payload = main
        else:
            hist, payload, moment = got
            pays.append(payload)
            moms.append(moment)

    packed, loc = lax.optimization_barrier((packed, loc))
    shares = lax.all_to_all(packed.reshape(ring, 512 // ring, 2 * rank), "blk", 0, 0, tiled=True)
    sums = call(sum_kernel, shape(shares.shape, BF16), [shares])
    sums = lax.all_to_all(sums, "blk", 0, 0, tiled=True).reshape(512, 2 * rank)
    place = jnp.stack([lax.axis_index("region"), device % 2]).astype(jnp.int32)
    halves = call(halves_kernel, shape((regions, 256 + 2 * rank, 2 * rank), BF16), [sums, coupling], [place])
    halves = lax.all_to_all(halves, "region", 0, 0, tiled=True)
    others = swap_cores(halves)

    currents = call(
        functools.partial(finish_kernel, steps, farp),
        shape((steps, blocks, pulses, rows), BF16),
        [halves, others, *pays, loc],
        [place],
        scratch=[
            pltpu.VMEM((regions, 512, 2 * rank), BF16),
            pltpu.VMEM((regions, 4 * rank, 2 * rank), BF16),
            pltpu.VMEM(((depth + steps) * regions, pulses, 2 * rank), BF16),
            pltpu.VMEM(((depth + steps) * regions, pulses, 2 * rank), BF16),
            pltpu.VMEM((regions, steps * rank, rank), BF16),
            pltpu.VMEM((regions, 8 * rank, rank), BF16),
            pltpu.VMEM((regions, pulses, steps * rank), BF16),
            pltpu.VMEM((steps * pulses, steps * rank), BF16),
            pltpu.VMEM((2 * regions, 128), jnp.int32),
            pltpu.SMEM((2 * regions, 128), jnp.int32),
            pltpu.SemaphoreType.DMA,
        ],
    )
    return currents[:, None]


def solution(mesh):
    in_specs = (
        P(None, "region", "blk", None, None),
        P(None, "region", "blk", None, None),
        P("region", "blk", None, None),
        P("region", "blk", None, None, None),
        P("region", "blk", None),
        P("region", "blk", None),
        P("region", None),
        P("region", "blk", None, None),
        P("region", "blk", None, None),
        P("region", None),
        P("region", None),
        P("region", None, None, None),
    )
    out_specs = P(None, "region", "blk", None, None)
    return jax.shard_map(on_device, mesh=mesh, in_specs=in_specs, out_specs=out_specs, check_vma=False)
```

```python
import functools

import jax
import jax.numpy as jnp
from jax import lax
from jax.experimental import pallas as pl
from jax.experimental.pallas import tpu as pltpu
from jax.sharding import PartitionSpec as P

SPAN = 2
TOGETHER = 4
VMEM_LIMIT = 12 * 2**20
F32 = jnp.float32
BF16 = jnp.bfloat16


def dot(a, b):
    return jnp.dot(a, b, preferred_element_type=F32)


def in_vmem(x):
    return pltpu.with_memory_space_constraint(x, pltpu.VMEM)


def in_hbm(x):
    return pltpu.with_memory_space_constraint(x, pltpu.HBM)


def call(kernel, out_shape, vmem_args, smem_args=(), scratch=(), aliases=None, flops=0, fetch=False):
    specs = [pl.BlockSpec(memory_space=pltpu.SMEM)] * len(smem_args)
    for arg in vmem_args:
        if fetch:
            specs.append(pl.BlockSpec(arg.shape, lambda i, n=arg.ndim: (0,) * n))
        else:
            specs.append(pl.BlockSpec(memory_space=pltpu.VMEM))
    return pl.pallas_call(
        kernel,
        grid=(1,) if fetch else (),
        out_shape=out_shape,
        in_specs=specs,
        out_specs=jax.tree.map(lambda _: pl.BlockSpec(memory_space=pltpu.VMEM), out_shape),
        scratch_shapes=list(scratch),
        input_output_aliases=aliases or {},
        compiler_params=pltpu.CompilerParams(vmem_limit_bytes=VMEM_LIMIT),
        cost_estimate=pl.CostEstimate(flops=flops, bytes_accessed=1 << 20, transcendentals=0),
    )(*smem_args, *vmem_args)


def shape(dims, dtype):
    return jax.ShapeDtypeStruct(dims, dtype)


def swap_cores(value):
    n = lax.axis_size("blk")
    return lax.ppermute(value, "blk", [(i, i ^ 1) for i in range(n)])


def paired(value, wanted, by):
    chips = lax.axis_size("blk") // 2
    pairs = []
    for c in range(chips - by):
        if wanted(c):
            for core in range(2):
                low, high = 2 * c + core, 2 * (c + by) + core
                pairs += [(low, high), (high, low)]
    return lax.ppermute(value, "blk", pairs)


def even_pairs(value):
    return paired(value, lambda c: c % 2 == 0, 1)


def odd_pairs(value):
    return paired(value, lambda c: c % 2 == 1, 1)


def window(value, beside, short=False):
    if short:
        near = even_pairs(value)
        last = paired(value, lambda c: c % 4 < 2, 2)
        other = odd_pairs(value)
        passed = paired(value, lambda c: c % 4 >= 2, 2)
        _, made = beside(None)
        passed, made = lax.optimization_barrier((passed, made))
    else:
        other = odd_pairs(value)
        near = even_pairs(value)
        other, made = beside(other)
        passed = odd_pairs(near)
        last = even_pairs(other)
        last, made = lax.optimization_barrier((last, made))
    direct = [value, near, other, last, passed]
    return direct + [swap_cores(v) for v in direct], made


def index_kernel(device_ref, cols_ref, delay_ref, slot_ref, *refs):
    count = (len(refs) - 4) // 2
    code_ref, off_ref, list_ref = refs[count : count + 3]
    sems = refs[-1]
    copies = [pltpu.make_async_copy(refs[i], refs[count + 3 + i], sems.at[i]) for i in range(count)]
    for copy in copies:
        copy.start()
    blocks, near = cols_ref.shape
    chip, core = device_ref[0] // 2, device_ref[0] % 2
    base = (chip - SPAN) * 2 * blocks
    top = (2 * SPAN + 1) * 2 * blocks - 1

    def row(b, spot):
        def one(j, spot):
            at = b * near + j
            local = jnp.clip(slot_ref[0, cols_ref[b, j]] - base, 0, top)
            delay = delay_ref[b, j]
            code_ref[at] = local * 8 + delay
            list_ref[spot] = at * 128 + local
            return spot + jnp.where(delay == 1, 1, 0)

        spot = lax.fori_loop(0, near, one, spot, unroll=8)
        list_ref[spot] = b * near * 128 + top + 1
        return spot + spot % 2

    spot = lax.fori_loop(0, blocks, row, 0)
    for i in range(2 * TOGETHER):
        list_ref[spot + i] = top + 1
    list_ref[list_ref.shape[0] - 1] = (spot + 2 * TOGETHER - 1) // (2 * TOGETHER)
    odd = jnp.where(chip % 2 == 0, 1, -1)
    two = jnp.where(chip % 4 < 2, 2, -2)
    for first, far in ((0, 2 * odd), (10, two)):
        for i, rel in enumerate((0, odd, -odd, far, -far)):
            off_ref[first + i] = ((rel + SPAN) * 2 + core) * blocks
            off_ref[first + i + 5] = ((rel + SPAN) * 2 + 1 - core) * blocks
    for copy in copies:
        copy.wait()


def start_kernel(past_ref, fin_ref, sinv_ref, fout_ref, coup_ref, pair_ref, delay_ref, pay_ref, mom_ref, send_ref):
    depth, blocks, pulses, _ = past_ref.shape
    rank = fin_ref.shape[1]
    farp = coup_ref.shape[0]
    for p in range(8):
        if p < farp:
            slab = coup_ref[p].astype(BF16)
        elif p == 7:
            row = lax.broadcasted_iota(jnp.int32, (rank, rank), 0)
            rest = jnp.zeros((1, rank - farp), jnp.int32)
            pair, delay = (jnp.concatenate([ref[...], rest], axis=1) for ref in (pair_ref, delay_ref))
            ints = jnp.where(row == 0, pair, jnp.where(row == 1, delay, 0))
            slab = ints.astype(F32).astype(BF16)
        else:
            slab = jnp.zeros((rank, rank), BF16)
        at, side = (p % 4) * rank, (p // 4) * rank
        send_ref[at : at + rank, side : side + rank] = slab
    total = jnp.zeros(mom_ref.shape, F32)
    for b in range(blocks):
        response = dot(fin_ref[b], sinv_ref[b]).astype(BF16)
        rows = [past_ref[0, b], response] + [past_ref[k, b] for k in range(1, depth)]
        whole = jnp.concatenate(rows, axis=0)
        pay_ref[b] = whole
        total = total + dot(whole, fout_ref[b])
    mom_ref[...] = total


def near_sum(step, b, rows, code_ref, tiles_ref, hist_ref, early=False):
    near = tiles_ref.shape[1]
    per_time = hist_ref.shape[0] // 4

    def source(at):
        code = code_ref[at]
        delay, local = code & 7, code >> 3
        if early:
            local = jnp.where(delay == 1, per_time - 1, local)
        return hist_ref[((step - delay) & 3) * per_time + local, :rows, :]

    acc = jnp.zeros((rows, tiles_ref.shape[3]), F32)
    for j in range(0, near, 2):
        at = b * near + j
        both = jnp.concatenate([source(at), source(at + 1)], axis=1)
        tile = tiles_ref[b, j : j + 2].reshape(-1, tiles_ref.shape[3])
        acc = acc + dot(both, tile)
    return acc


def early_kernel(step, code_ref, tiles_ref, hist_ref, acc_ref):
    def row(b, _):
        acc_ref[b] = near_sum(step, b, acc_ref.shape[1], code_ref, tiles_ref, hist_ref, early=True)
        return 0

    lax.fori_loop(0, acc_ref.shape[0], row, 0)


def step_kernel(step, last, packs, *refs):
    refs = list(refs)
    code_ref, off_ref, list_ref = refs[:3]
    pieces = refs[3:13]
    tiles_ref, inc_ref, sinv_ref, fout_ref = refs[13:17]
    rest = refs[17:]
    moms = []
    if step > 0:
        early_ref, sum_ref = rest[1], rest[-1]
        rest = rest[2:-1]
    if packs:
        moms, rest = rest[:packs], rest[packs:]
    blocks, near = tiles_ref.shape[:2]
    pulses = inc_ref.shape[2]
    if last:
        loc_ref, hist_ref = rest
        rows = pulses
    else:
        hist_ref, pay_ref, mom_ref = rest[:3]
        rows = pay_ref.shape[1]
    per_time = hist_ref.shape[0] // 4
    held = hist_ref.shape[1]

    if step == 0:
        for k in range(1, 4):
            hist_ref[pl.ds((3 - k) * per_time, per_time), pulses:held, :] = jnp.zeros(
                (per_time, held - pulses, hist_ref.shape[2]), BF16
            )
        for k in range(4):
            hist_ref[(k + 1) * per_time - 1] = jnp.zeros(hist_ref.shape[1:], BF16)
    for i, piece in enumerate(pieces):
        off = off_ref[i + 10] if last else off_ref[i]
        if step == 0:
            hist_ref[pl.ds(3 * per_time + off, blocks), :, :] = piece[:, :held, :]
            for k in range(1, 4):
                row = held + (k - 1) * pulses
                hist_ref[pl.ds((3 - k) * per_time + off, blocks), :pulses, :] = piece[:, row : row + pulses, :]
        else:
            hist_ref[pl.ds(((step - 1) % 4) * per_time + off, blocks), :rows, :] = piece[...]

    if step > 0:
        newest = ((step - 1) & 3) * per_time
        sum_ref[...] = early_ref[...]

        def turn(i, _):
            sums = []
            for pair in range(TOGETHER):
                one, two = (list_ref[(i * TOGETHER + pair) * 2 + k] for k in range(2))
                both = jnp.concatenate([hist_ref[newest + (c & 127), :rows, :] for c in (one, two)], axis=1)
                at = [c >> 7 for c in (one, two)]
                tile = jnp.concatenate([tiles_ref[t // near, t % near] for t in at], axis=0)
                sums.append((at[0] // near, dot(both, tile)))
            for b, value in sums:
                sum_ref[b] += value
            return 0

        lax.fori_loop(0, list_ref[list_ref.shape[0] - 1], turn, 0)

    def row(b, total):
        if step == 0:
            acc = near_sum(step, b, rows, code_ref, tiles_ref, hist_ref)
        else:
            acc = sum_ref[b]
        main = inc_ref[step, b].astype(F32) - acc[:pulses]
        driven = main if last else jnp.concatenate([main, -acc[pulses:]], axis=0)
        current = dot(driven.astype(BF16), sinv_ref[b])
        if last:
            loc_ref[b] = current
            return total
        rounded = current.astype(BF16)
        pay_ref[b] = rounded
        return total + dot(rounded, fout_ref[b])

    start = jnp.zeros((rows, fout_ref.shape[2]), F32)
    total = lax.fori_loop(0, blocks, row, start, unroll=step > 0)
    if last:
        return
    if not packs:
        mom_ref[...] = total
        return
    main_ref = rest[3]
    main_ref[...] = pay_ref[:, :pulses, :]
    listed = [m[...] for m in moms] + [total[:pulses]]
    every = jnp.concatenate(listed, axis=0).astype(BF16)
    half, rank = every.shape[0] // 2, every.shape[1]
    mom_ref[:half, :rank] = every[:half]
    mom_ref[:half, rank:] = every[half:]
    mom_ref[half:, :] = jnp.zeros((mom_ref.shape[0] - half, mom_ref.shape[1]), BF16)


def sum_kernel(in_ref, out_ref):
    total = in_ref[0].astype(F32)
    for i in range(1, in_ref.shape[0]):
        total = total + in_ref[i].astype(F32)
    for i in range(out_ref.shape[0]):
        out_ref[i] = total.astype(BF16)


def halves_kernel(place_ref, sums_ref, coup_ref, out_ref):
    core = place_ref[1]
    part = coup_ref.shape[0] // 2
    used = out_ref.shape[1] - part
    for i, ref, rows in ((0, sums_ref, used), (used, coup_ref, part)):
        half = ref[pl.ds(pl.multiple_of(core * rows, 16), rows), :]
        for g in range(out_ref.shape[0]):
            out_ref[g, i : i + rows, :] = half


def finish_kernel(steps, farp, place_ref, mine_ref, other_ref, *refs):
    pays = refs[:steps]
    loc_ref, out_ref, got_ref, coup_ref, low_ref, high_ref, qrev_ref, c_ref, bl_ref, a_ref, ints_ref, num_ref, sem = refs[steps:]
    regions = got_ref.shape[0]
    depth = 4
    blocks, pulses = loc_ref.shape[:2]
    rank = coup_ref.shape[2] // 2
    held = pulses + rank
    first = held + (depth - 1) * pulses
    half = (first + (steps - 2) * held + pulses) // 2

    for ref, core in ((mine_ref, place_ref[1]), (other_ref, 1 - place_ref[1])):
        for whole, at in ((got_ref, 0), (coup_ref, got_ref.shape[1] // 2)):
            rows = whole.shape[1] // 2
            whole[:, pl.ds(pl.multiple_of(core * rows, 16), rows), :] = ref[:, at : at + rows, :]

    ints_ref[...] = jnp.zeros(ints_ref.shape, jnp.int32)
    for g in range(regions):
        numbers = coup_ref[g, 3 * rank : 3 * rank + 16, rank:].astype(F32).astype(jnp.int32)
        ints_ref[2 * g : 2 * g + 2, :rank] = numbers[:2]
    copy = pltpu.make_async_copy(ints_ref, num_ref, sem)
    copy.start()

    def rows_of(g, at, count):
        parts = []
        for r in range(at, at + count, 16):
            side, row = divmod(r, half)
            parts.append(got_ref[g, row : row + 16, side * rank : (side + 1) * rank])
        return jnp.concatenate(parts, axis=0)

    def keep(time, g, value):
        low_ref[(time + depth) * regions + g, :, :rank] = value
        high_ref[(time + depth) * regions + g, :, rank:] = value

    def source(n, g, q):
        return (n - num_ref[2 * g + 1, q] + depth) * regions + num_ref[2 * g, q]

    low_ref[...] = jnp.zeros(low_ref.shape, BF16)
    high_ref[...] = jnp.zeros(high_ref.shape, BF16)
    bl_ref[...] = jnp.zeros(bl_ref.shape, BF16)
    a_ref[...] = jnp.zeros(a_ref.shape, BF16)
    for g in range(regions):
        keep(-1, g, rows_of(g, 0, pulses))
        for k in range(1, depth):
            keep(-1 - k, g, rows_of(g, held + (k - 1) * pulses, pulses))
        for lag in range(steps - 1):
            at = pulses if lag == 0 else first + (lag - 1) * held + pulses
            spot = (steps - 2 - lag) * rank
            qrev_ref[g, spot : spot + rank, :] = rows_of(g, at, rank)
        qrev_ref[g, (steps - 1) * rank :, :] = jnp.zeros((rank, rank), BF16)
        for p in range(8):
            c_ref[g, p * rank : (p + 1) * rank, :] = (
                coup_ref[g, (p % 4) * rank : (p % 4 + 1) * rank, (p // 4) * rank : (p // 4 + 1) * rank]
                if p < farp
                else jnp.zeros((rank, rank), BF16)
            )

    copy.wait()
    for n in range(steps):
        blended = []
        for g in range(regions):
            acc = jnp.zeros((pulses, rank), F32)
            for p in range(0, farp, 4):
                lanes = []
                for q in range(p, min(p + 4, farp), 2):
                    part = low_ref[source(n, g, q)]
                    if q + 1 < farp:
                        part = part + high_ref[source(n, g, q + 1)]
                    lanes.append(part)
                lhs = jnp.concatenate(lanes, axis=1)
                acc = acc + dot(lhs, c_ref[g, p * rank : p * rank + lhs.shape[1], :])
            blended.append(acc.astype(BF16))
        for g in range(regions):
            bl_ref[g, :, n * rank : (n + 1) * rank] = blended[g]
        if n < steps - 1:
            depth_k = 2 * rank * ((n + 2) // 2)
            at = first + n * held
            spot = (steps - 2 - n) * rank
            for g in range(regions):
                change = dot(bl_ref[g, :, :depth_k], qrev_ref[g, spot : spot + depth_k, :])
                keep(n, g, (rows_of(g, at, pulses).astype(F32) - change).astype(BF16))

    mine = place_ref[0]
    for n in range(steps):
        a_ref[n * pulses : (n + 1) * pulses, (steps - 1 - n) * rank :] = bl_ref[mine, :, : (n + 1) * rank]
    for b in range(blocks):
        response = jnp.concatenate([pays[k][b, pulses : pulses + rank, :] for k in reversed(range(steps))], axis=0)
        far = dot(a_ref[...], response)
        for n in range(steps):
            local = loc_ref[b] if n == steps - 1 else pays[n + 1][b, :pulses, :].astype(F32)
            out_ref[n, b] = (local - far[n * pulses : (n + 1) * pulses]).astype(BF16)


def on_device(
    incident,
    past_currents,
    self_inverse,
    near_tiles,
    near_cols,
    near_delay,
    block_slot,
    far_out,
    far_in,
    far_pairs,
    far_delay,
    far_coupling,
):
    steps, _, blocks, pulses, rows = incident.shape
    depth = past_currents.shape[0]
    near = near_cols.shape[2]
    farp, rank = far_coupling.shape[1:3]
    regions = lax.axis_size("region")
    ring = lax.axis_size("blk")
    device = lax.axis_index("blk")
    held = pulses + rank
    near_blocks = (2 * SPAN + 1) * 2 * blocks + 1

    past, fin = past_currents[:, 0], far_in[0]

    first = held + (depth - 1) * pulses
    payload, moment, coupling = call(
        start_kernel,
        (
            shape((blocks, first, rows), BF16),
            shape((first, rank), F32),
            shape((4 * rank, 2 * rank), BF16),
        ),
        [in_hbm(x) for x in (past, fin, self_inverse[0], far_out[0], far_coupling[0], far_pairs, far_delay)],
        fetch=True,
    )
    fetched = [near_tiles[0], incident[:, 0], self_inverse[0], far_out[0]]
    code, offsets, late, tiles, inc, sinv, fout = pl.pallas_call(
        index_kernel,
        out_shape=(
            shape((blocks * near,), jnp.int32),
            shape((20,), jnp.int32),
            shape((blocks * (near + 1) + 2 * TOGETHER + 8,), jnp.int32),
            *(shape(x.shape, x.dtype) for x in fetched),
        ),
        in_specs=[pl.BlockSpec(memory_space=pltpu.SMEM)] * 4 + [pl.BlockSpec(memory_space=pltpu.HBM)] * 4,
        out_specs=(pl.BlockSpec(memory_space=pltpu.SMEM),) * 3 + (pl.BlockSpec(memory_space=pltpu.VMEM),) * 4,
        scratch_shapes=[pltpu.SemaphoreType.DMA((4,))],
        compiler_params=pltpu.CompilerParams(vmem_limit_bytes=VMEM_LIMIT),
        cost_estimate=pl.CostEstimate(flops=0, bytes_accessed=1 << 24, transcendentals=0),
    )(
        device.astype(jnp.int32).reshape(1),
        near_cols[0],
        near_delay[0],
        block_slot,
        *(in_hbm(x) for x in fetched),
    )
    pays, moms = [payload], [moment]
    hist = None
    hist_shape = shape((4 * near_blocks, held, rows), BF16)
    flops = 2 * blocks * near * held * rows * rows
    for n in range(steps):
        last = n == steps - 1
        packs = len(moms) if n == steps - 2 else 0
        tail, aliases, scratch = [], {}, []
        if n == 0:
            pieces, code = window(payload, lambda arrived: (arrived, code))
        else:
            wide = pulses if last else held

            def beside(arrived):
                arrived, codes = (None, code) if last else lax.optimization_barrier((arrived, code))
                early = call(
                    functools.partial(early_kernel, n),
                    shape((blocks, wide, rows), F32),
                    [in_vmem(tiles), in_vmem(hist)],
                    [codes],
                    flops=flops,
                )
                return arrived, early

            pieces, early = window(payload, beside, last)
            tail = [in_vmem(hist), early]
            scratch = [pltpu.VMEM((blocks, wide, rows), F32)]
        args = pieces + [in_vmem(tiles), inc, sinv, fout] + tail
        if n > 0:
            aliases = {3 + len(args) - 2: 1 if last else 0}
        loc_shape = shape((blocks, pulses, rows), F32)
        if last:
            outs = (loc_shape, hist_shape)
        elif packs:
            args += moms
            outs = (
                hist_shape,
                shape((blocks, held, rows), BF16),
                shape((512, 2 * rank), BF16),
                shape((blocks, pulses, rows), BF16),
            )
        else:
            outs = (hist_shape, shape((blocks, held, rows), BF16), shape((held, rank), F32))
        got = call(
            functools.partial(step_kernel, n, last, packs),
            outs,
            args,
            [code, offsets, late],
            scratch=scratch,
            aliases=aliases,
            flops=flops,
        )
        if last:
            loc = got[0]
        elif packs:
            hist, payload, packed, main = got
            pays.append(payload)
            payload = main
        else:
            hist, payload, moment = got
            pays.append(payload)
            moms.append(moment)

    packed, loc = lax.optimization_barrier((packed, loc))
    shares = lax.all_to_all(packed.reshape(ring, 512 // ring, 2 * rank), "blk", 0, 0, tiled=True)
    sums = call(sum_kernel, shape(shares.shape, BF16), [shares])
    sums = lax.all_to_all(sums, "blk", 0, 0, tiled=True).reshape(512, 2 * rank)
    moment_rows = first + (steps - 2) * held + pulses
    used = -(-moment_rows // 64) * 16
    place = jnp.stack([lax.axis_index("region"), device % 2]).astype(jnp.int32)
    halves = call(halves_kernel, shape((regions, used + 2 * rank, 2 * rank), BF16), [sums, coupling], [place])
    halves = lax.all_to_all(halves, "region", 0, 0, tiled=True)
    others = swap_cores(halves)

    currents = call(
        functools.partial(finish_kernel, steps, farp),
        shape((steps, blocks, pulses, rows), BF16),
        [halves, others, *pays, loc],
        [place],
        scratch=[
            pltpu.VMEM((regions, 2 * used, 2 * rank), BF16),
            pltpu.VMEM((regions, 4 * rank, 2 * rank), BF16),
            pltpu.VMEM(((depth + steps) * regions, pulses, 2 * rank), BF16),
            pltpu.VMEM(((depth + steps) * regions, pulses, 2 * rank), BF16),
            pltpu.VMEM((regions, steps * rank, rank), BF16),
            pltpu.VMEM((regions, 8 * rank, rank), BF16),
            pltpu.VMEM((regions, pulses, steps * rank), BF16),
            pltpu.VMEM((steps * pulses, steps * rank), BF16),
            pltpu.VMEM((2 * regions, 128), jnp.int32),
            pltpu.SMEM((2 * regions, 128), jnp.int32),
            pltpu.SemaphoreType.DMA,
        ],
    )
    return currents[:, None]


def solution(mesh):
    in_specs = (
        P(None, "region", "blk", None, None),
        P(None, "region", "blk", None, None),
        P("region", "blk", None, None),
        P("region", "blk", None, None, None),
        P("region", "blk", None),
        P("region", "blk", None),
        P("region", None),
        P("region", "blk", None, None),
        P("region", "blk", None, None),
        P("region", None),
        P("region", None),
        P("region", None, None, None),
    )
    out_specs = P(None, "region", "blk", None, None)
    return jax.shard_map(on_device, mesh=mesh, in_specs=in_specs, out_specs=out_specs, check_vma=False)
```

```python
import functools

import jax
import jax.numpy as jnp
from jax import lax
from jax.experimental import pallas as pl
from jax.experimental.pallas import tpu as pltpu
from jax.sharding import PartitionSpec as P

SPAN = 2
TOGETHER = 8
VMEM_LIMIT = 12 * 2**20
F32 = jnp.float32
BF16 = jnp.bfloat16


def dot(a, b):
    return jnp.dot(a, b, preferred_element_type=F32)


def in_vmem(x):
    return pltpu.with_memory_space_constraint(x, pltpu.VMEM)


def in_hbm(x):
    return pltpu.with_memory_space_constraint(x, pltpu.HBM)


def call(kernel, out_shape, vmem_args, smem_args=(), scratch=(), aliases=None, flops=0, fetch=False):
    specs = [pl.BlockSpec(memory_space=pltpu.SMEM)] * len(smem_args)
    for arg in vmem_args:
        if fetch:
            specs.append(pl.BlockSpec(arg.shape, lambda i, n=arg.ndim: (0,) * n))
        else:
            specs.append(pl.BlockSpec(memory_space=pltpu.VMEM))
    return pl.pallas_call(
        kernel,
        grid=(1,) if fetch else (),
        out_shape=out_shape,
        in_specs=specs,
        out_specs=jax.tree.map(lambda _: pl.BlockSpec(memory_space=pltpu.VMEM), out_shape),
        scratch_shapes=list(scratch),
        input_output_aliases=aliases or {},
        compiler_params=pltpu.CompilerParams(vmem_limit_bytes=VMEM_LIMIT),
        cost_estimate=pl.CostEstimate(flops=flops, bytes_accessed=1 << 20, transcendentals=0),
    )(*smem_args, *vmem_args)


def shape(dims, dtype):
    return jax.ShapeDtypeStruct(dims, dtype)


def swap_cores(value):
    n = lax.axis_size("blk")
    return lax.ppermute(value, "blk", [(i, i ^ 1) for i in range(n)])


def paired(value, wanted, by):
    chips = lax.axis_size("blk") // 2
    pairs = []
    for c in range(chips - by):
        if wanted(c):
            for core in range(2):
                low, high = 2 * c + core, 2 * (c + by) + core
                pairs += [(low, high), (high, low)]
    return lax.ppermute(value, "blk", pairs)


def even_pairs(value):
    return paired(value, lambda c: c % 2 == 0, 1)


def odd_pairs(value):
    return paired(value, lambda c: c % 2 == 1, 1)


def window(value, beside, short=False):
    if short:
        near = even_pairs(value)
        last = paired(value, lambda c: c % 4 < 2, 2)
        other = odd_pairs(value)
        passed = paired(value, lambda c: c % 4 >= 2, 2)
        _, made = beside(None)
        passed, made = lax.optimization_barrier((passed, made))
    else:
        other = odd_pairs(value)
        near = even_pairs(value)
        other, made = beside(other)
        passed = odd_pairs(near)
        last = even_pairs(other)
        last, made = lax.optimization_barrier((last, made))
    direct = [value, near, other, last, passed]
    return direct + [swap_cores(v) for v in direct], made


def index_kernel(device_ref, cols_ref, delay_ref, slot_ref, *refs):
    count = (len(refs) - 4) // 2
    code_ref, off_ref, list_ref = refs[count : count + 3]
    sems = refs[-1]
    copies = [pltpu.make_async_copy(refs[i], refs[count + 3 + i], sems.at[i]) for i in range(count)]
    for copy in copies:
        copy.start()
    blocks, near = cols_ref.shape
    chip, core = device_ref[0] // 2, device_ref[0] % 2
    base = (chip - SPAN) * 2 * blocks
    top = (2 * SPAN + 1) * 2 * blocks - 1

    def row(b, spot):
        def one(j, spot):
            at = b * near + j
            local = jnp.clip(slot_ref[0, cols_ref[b, j]] - base, 0, top)
            delay = delay_ref[b, j]
            code_ref[at] = local * 8 + delay
            list_ref[spot] = at * 128 + local
            return spot + jnp.where(delay == 1, 1, 0)

        spot = lax.fori_loop(0, near, one, spot, unroll=8)
        list_ref[spot] = b * near * 128 + top + 1
        return spot + spot % 2

    spot = lax.fori_loop(0, blocks, row, 0)
    for i in range(2 * TOGETHER):
        list_ref[spot + i] = top + 1
    list_ref[list_ref.shape[0] - 1] = (spot + 2 * TOGETHER - 1) // (2 * TOGETHER)
    odd = jnp.where(chip % 2 == 0, 1, -1)
    two = jnp.where(chip % 4 < 2, 2, -2)
    for first, far in ((0, 2 * odd), (10, two)):
        for i, rel in enumerate((0, odd, -odd, far, -far)):
            off_ref[first + i] = ((rel + SPAN) * 2 + core) * blocks
            off_ref[first + i + 5] = ((rel + SPAN) * 2 + 1 - core) * blocks
    for copy in copies:
        copy.wait()


def start_kernel(past_ref, fin_ref, sinv_ref, fout_ref, coup_ref, pair_ref, delay_ref, pay_ref, mom_ref, send_ref):
    depth, blocks, pulses, _ = past_ref.shape
    rank = fin_ref.shape[1]
    farp = coup_ref.shape[0]
    for p in range(8):
        if p < farp:
            slab = coup_ref[p].astype(BF16)
        elif p == 7:
            row = lax.broadcasted_iota(jnp.int32, (rank, rank), 0)
            rest = jnp.zeros((1, rank - farp), jnp.int32)
            pair, delay = (jnp.concatenate([ref[...], rest], axis=1) for ref in (pair_ref, delay_ref))
            ints = jnp.where(row == 0, pair, jnp.where(row == 1, delay, 0))
            slab = ints.astype(F32).astype(BF16)
        else:
            slab = jnp.zeros((rank, rank), BF16)
        at, side = (p % 4) * rank, (p // 4) * rank
        send_ref[at : at + rank, side : side + rank] = slab
    total = jnp.zeros(mom_ref.shape, F32)
    for b in range(blocks):
        response = dot(fin_ref[b], sinv_ref[b]).astype(BF16)
        rows = [past_ref[0, b], response] + [past_ref[k, b] for k in range(1, depth)]
        whole = jnp.concatenate(rows, axis=0)
        pay_ref[b] = whole
        total = total + dot(whole, fout_ref[b])
    mom_ref[...] = total


def near_sum(step, b, rows, code_ref, tiles_ref, hist_ref, early=False):
    near = tiles_ref.shape[1]
    per_time = hist_ref.shape[0] // 4

    def source(at):
        code = code_ref[at]
        delay, local = code & 7, code >> 3
        if early:
            local = jnp.where(delay == 1, per_time - 1, local)
        return hist_ref[((step - delay) & 3) * per_time + local, :rows, :]

    acc = jnp.zeros((rows, tiles_ref.shape[3]), F32)
    for j in range(0, near, 2):
        at = b * near + j
        both = jnp.concatenate([source(at), source(at + 1)], axis=1)
        tile = tiles_ref[b, j : j + 2].reshape(-1, tiles_ref.shape[3])
        acc = acc + dot(both, tile)
    return acc


def early_kernel(step, code_ref, tiles_ref, hist_ref, acc_ref):
    def row(b, _):
        acc_ref[b] = near_sum(step, b, acc_ref.shape[1], code_ref, tiles_ref, hist_ref, early=True)
        return 0

    lax.fori_loop(0, acc_ref.shape[0], row, 0)


def step_kernel(step, last, packs, *refs):
    refs = list(refs)
    code_ref, off_ref, list_ref = refs[:3]
    pieces = refs[3:13]
    tiles_ref, inc_ref, sinv_ref, fout_ref = refs[13:17]
    rest = refs[17:]
    moms = []
    if step > 0:
        early_ref, sum_ref = rest[1], rest[-1]
        rest = rest[2:-1]
    if packs:
        moms, rest = rest[:packs], rest[packs:]
    blocks, near = tiles_ref.shape[:2]
    pulses = inc_ref.shape[2]
    if last:
        loc_ref, hist_ref = rest
        rows = pulses
    else:
        hist_ref, pay_ref, mom_ref = rest[:3]
        rows = pay_ref.shape[1]
    per_time = hist_ref.shape[0] // 4
    held = hist_ref.shape[1]

    if step == 0:
        for k in range(1, 4):
            hist_ref[pl.ds((3 - k) * per_time, per_time), pulses:held, :] = jnp.zeros(
                (per_time, held - pulses, hist_ref.shape[2]), BF16
            )
        for k in range(4):
            hist_ref[(k + 1) * per_time - 1] = jnp.zeros(hist_ref.shape[1:], BF16)
    for i, piece in enumerate(pieces):
        off = off_ref[i + 10] if last else off_ref[i]
        if step == 0:
            hist_ref[pl.ds(3 * per_time + off, blocks), :, :] = piece[:, :held, :]
            for k in range(1, 4):
                row = held + (k - 1) * pulses
                hist_ref[pl.ds((3 - k) * per_time + off, blocks), :pulses, :] = piece[:, row : row + pulses, :]
        else:
            hist_ref[pl.ds(((step - 1) % 4) * per_time + off, blocks), :rows, :] = piece[...]

    if step > 0:
        newest = ((step - 1) & 3) * per_time
        sum_ref[...] = early_ref[...]

        def turn(i, _):
            sums = []
            for pair in range(TOGETHER):
                one, two = (list_ref[(i * TOGETHER + pair) * 2 + k] for k in range(2))
                both = jnp.concatenate([hist_ref[newest + (c & 127), :rows, :] for c in (one, two)], axis=1)
                at = [c >> 7 for c in (one, two)]
                tile = jnp.concatenate([tiles_ref[t // near, t % near] for t in at], axis=0)
                sums.append((at[0] // near, dot(both, tile)))
            for b, value in sums:
                sum_ref[b] += value
            return 0

        lax.fori_loop(0, list_ref[list_ref.shape[0] - 1], turn, 0)

    def row(b, total):
        if step == 0:
            acc = near_sum(step, b, rows, code_ref, tiles_ref, hist_ref)
        else:
            acc = sum_ref[b]
        main = inc_ref[step, b].astype(F32) - acc[:pulses]
        driven = main if last else jnp.concatenate([main, -acc[pulses:]], axis=0)
        current = dot(driven.astype(BF16), sinv_ref[b])
        if last:
            loc_ref[b] = current
            return total
        rounded = current.astype(BF16)
        pay_ref[b] = rounded
        return total + dot(rounded, fout_ref[b])

    start = jnp.zeros((rows, fout_ref.shape[2]), F32)
    total = lax.fori_loop(0, blocks, row, start, unroll=step > 0)
    if last:
        return
    if not packs:
        mom_ref[...] = total
        return
    main_ref = rest[3]
    main_ref[...] = pay_ref[:, :pulses, :]
    listed = [m[...] for m in moms] + [total[:pulses]]
    every = jnp.concatenate(listed, axis=0).astype(BF16)
    half, rank = every.shape[0] // 2, every.shape[1]
    mom_ref[:half, :rank] = every[:half]
    mom_ref[:half, rank:] = every[half:]
    mom_ref[half:, :] = jnp.zeros((mom_ref.shape[0] - half, mom_ref.shape[1]), BF16)


def sum_kernel(in_ref, out_ref):
    total = in_ref[0].astype(F32)
    for i in range(1, in_ref.shape[0]):
        total = total + in_ref[i].astype(F32)
    for i in range(out_ref.shape[0]):
        out_ref[i] = total.astype(BF16)


def halves_kernel(place_ref, sums_ref, coup_ref, out_ref):
    core = place_ref[1]
    part = coup_ref.shape[0] // 2
    used = out_ref.shape[1] - part
    for i, ref, rows in ((0, sums_ref, used), (used, coup_ref, part)):
        half = ref[pl.ds(pl.multiple_of(core * rows, 16), rows), :]
        for g in range(out_ref.shape[0]):
            out_ref[g, i : i + rows, :] = half


def finish_kernel(steps, farp, place_ref, mine_ref, other_ref, *refs):
    pays = refs[:steps]
    loc_ref, out_ref, got_ref, coup_ref, low_ref, high_ref, qrev_ref, c_ref, bl_ref, a_ref, ints_ref, num_ref, sem = refs[steps:]
    regions = got_ref.shape[0]
    depth = 4
    blocks, pulses = loc_ref.shape[:2]
    rank = coup_ref.shape[2] // 2
    held = pulses + rank
    first = held + (depth - 1) * pulses
    half = (first + (steps - 2) * held + pulses) // 2

    for ref, core in ((mine_ref, place_ref[1]), (other_ref, 1 - place_ref[1])):
        for whole, at in ((got_ref, 0), (coup_ref, got_ref.shape[1] // 2)):
            rows = whole.shape[1] // 2
            whole[:, pl.ds(pl.multiple_of(core * rows, 16), rows), :] = ref[:, at : at + rows, :]

    ints_ref[...] = jnp.zeros(ints_ref.shape, jnp.int32)
    for g in range(regions):
        numbers = coup_ref[g, 3 * rank : 3 * rank + 16, rank:].astype(F32).astype(jnp.int32)
        ints_ref[2 * g : 2 * g + 2, :rank] = numbers[:2]
    copy = pltpu.make_async_copy(ints_ref, num_ref, sem)
    copy.start()

    def rows_of(g, at, count):
        parts = []
        for r in range(at, at + count, 16):
            side, row = divmod(r, half)
            parts.append(got_ref[g, row : row + 16, side * rank : (side + 1) * rank])
        return jnp.concatenate(parts, axis=0)

    def keep(time, g, value):
        low_ref[(time + depth) * regions + g, :, :rank] = value
        high_ref[(time + depth) * regions + g, :, rank:] = value

    def source(n, g, q):
        return (n - num_ref[2 * g + 1, q] + depth) * regions + num_ref[2 * g, q]

    low_ref[...] = jnp.zeros(low_ref.shape, BF16)
    high_ref[...] = jnp.zeros(high_ref.shape, BF16)
    bl_ref[...] = jnp.zeros(bl_ref.shape, BF16)
    a_ref[...] = jnp.zeros(a_ref.shape, BF16)
    for g in range(regions):
        keep(-1, g, rows_of(g, 0, pulses))
        for k in range(1, depth):
            keep(-1 - k, g, rows_of(g, held + (k - 1) * pulses, pulses))
        for lag in range(steps - 1):
            at = pulses if lag == 0 else first + (lag - 1) * held + pulses
            spot = (steps - 2 - lag) * rank
            qrev_ref[g, spot : spot + rank, :] = rows_of(g, at, rank)
        qrev_ref[g, (steps - 1) * rank :, :] = jnp.zeros((rank, rank), BF16)
        for p in range(8):
            c_ref[g, p * rank : (p + 1) * rank, :] = (
                coup_ref[g, (p % 4) * rank : (p % 4 + 1) * rank, (p // 4) * rank : (p // 4 + 1) * rank]
                if p < farp
                else jnp.zeros((rank, rank), BF16)
            )

    copy.wait()
    for n in range(steps):
        blended = []
        for g in range(regions):
            acc = jnp.zeros((pulses, rank), F32)
            for p in range(0, farp, 4):
                lanes = []
                for q in range(p, min(p + 4, farp), 2):
                    part = low_ref[source(n, g, q)]
                    if q + 1 < farp:
                        part = part + high_ref[source(n, g, q + 1)]
                    lanes.append(part)
                lhs = jnp.concatenate(lanes, axis=1)
                acc = acc + dot(lhs, c_ref[g, p * rank : p * rank + lhs.shape[1], :])
            blended.append(acc.astype(BF16))
        for g in range(regions):
            bl_ref[g, :, n * rank : (n + 1) * rank] = blended[g]
        if n < steps - 1:
            depth_k = 2 * rank * ((n + 2) // 2)
            at = first + n * held
            spot = (steps - 2 - n) * rank
            for g in range(regions):
                change = dot(bl_ref[g, :, :depth_k], qrev_ref[g, spot : spot + depth_k, :])
                keep(n, g, (rows_of(g, at, pulses).astype(F32) - change).astype(BF16))

    mine = place_ref[0]
    for n in range(steps):
        a_ref[n * pulses : (n + 1) * pulses, (steps - 1 - n) * rank :] = bl_ref[mine, :, : (n + 1) * rank]
    for b in range(blocks):
        response = jnp.concatenate([pays[k][b, pulses : pulses + rank, :] for k in reversed(range(steps))], axis=0)
        far = dot(a_ref[...], response)
        for n in range(steps):
            local = loc_ref[b] if n == steps - 1 else pays[n + 1][b, :pulses, :].astype(F32)
            out_ref[n, b] = (local - far[n * pulses : (n + 1) * pulses]).astype(BF16)


def on_device(
    incident,
    past_currents,
    self_inverse,
    near_tiles,
    near_cols,
    near_delay,
    block_slot,
    far_out,
    far_in,
    far_pairs,
    far_delay,
    far_coupling,
):
    steps, _, blocks, pulses, rows = incident.shape
    depth = past_currents.shape[0]
    near = near_cols.shape[2]
    farp, rank = far_coupling.shape[1:3]
    regions = lax.axis_size("region")
    ring = lax.axis_size("blk")
    device = lax.axis_index("blk")
    held = pulses + rank
    near_blocks = (2 * SPAN + 1) * 2 * blocks + 1

    past, fin = past_currents[:, 0], far_in[0]

    first = held + (depth - 1) * pulses
    payload, moment, coupling = call(
        start_kernel,
        (
            shape((blocks, first, rows), BF16),
            shape((first, rank), F32),
            shape((4 * rank, 2 * rank), BF16),
        ),
        [in_hbm(x) for x in (past, fin, self_inverse[0], far_out[0], far_coupling[0], far_pairs, far_delay)],
        fetch=True,
    )
    fetched = [near_tiles[0], incident[:, 0], self_inverse[0], far_out[0]]
    code, offsets, late, tiles, inc, sinv, fout = pl.pallas_call(
        index_kernel,
        out_shape=(
            shape((blocks * near,), jnp.int32),
            shape((20,), jnp.int32),
            shape((blocks * (near + 1) + 2 * TOGETHER + 8,), jnp.int32),
            *(shape(x.shape, x.dtype) for x in fetched),
        ),
        in_specs=[pl.BlockSpec(memory_space=pltpu.SMEM)] * 4 + [pl.BlockSpec(memory_space=pltpu.HBM)] * 4,
        out_specs=(pl.BlockSpec(memory_space=pltpu.SMEM),) * 3 + (pl.BlockSpec(memory_space=pltpu.VMEM),) * 4,
        scratch_shapes=[pltpu.SemaphoreType.DMA((4,))],
        compiler_params=pltpu.CompilerParams(vmem_limit_bytes=VMEM_LIMIT),
        cost_estimate=pl.CostEstimate(flops=0, bytes_accessed=1 << 24, transcendentals=0),
    )(
        device.astype(jnp.int32).reshape(1),
        near_cols[0],
        near_delay[0],
        block_slot,
        *(in_hbm(x) for x in fetched),
    )
    pays, moms = [payload], [moment]
    hist = None
    hist_shape = shape((4 * near_blocks, held, rows), BF16)
    flops = 2 * blocks * near * held * rows * rows
    for n in range(steps):
        last = n == steps - 1
        packs = len(moms) if n == steps - 2 else 0
        tail, aliases, scratch = [], {}, []
        if n == 0:
            pieces, code = window(payload, lambda arrived: (arrived, code))
        else:
            wide = pulses if last else held

            def beside(arrived):
                arrived, codes = (None, code) if last else lax.optimization_barrier((arrived, code))
                early = call(
                    functools.partial(early_kernel, n),
                    shape((blocks, wide, rows), F32),
                    [in_vmem(tiles), in_vmem(hist)],
                    [codes],
                    flops=flops,
                )
                return arrived, early

            pieces, early = window(payload, beside, last)
            tail = [in_vmem(hist), early]
            scratch = [pltpu.VMEM((blocks, wide, rows), F32)]
        args = pieces + [in_vmem(tiles), inc, sinv, fout] + tail
        if n > 0:
            aliases = {3 + len(args) - 2: 1 if last else 0}
        loc_shape = shape((blocks, pulses, rows), F32)
        if last:
            outs = (loc_shape, hist_shape)
        elif packs:
            args += moms
            outs = (
                hist_shape,
                shape((blocks, held, rows), BF16),
                shape((512, 2 * rank), BF16),
                shape((blocks, pulses, rows), BF16),
            )
        else:
            outs = (hist_shape, shape((blocks, held, rows), BF16), shape((held, rank), F32))
        got = call(
            functools.partial(step_kernel, n, last, packs),
            outs,
            args,
            [code, offsets, late],
            scratch=scratch,
            aliases=aliases,
            flops=flops,
        )
        if last:
            loc = got[0]
        elif packs:
            hist, payload, packed, main = got
            pays.append(payload)
            payload = main
        else:
            hist, payload, moment = got
            pays.append(payload)
            moms.append(moment)

    packed, loc = lax.optimization_barrier((packed, loc))
    shares = lax.all_to_all(packed.reshape(ring, 512 // ring, 2 * rank), "blk", 0, 0, tiled=True)
    sums = call(sum_kernel, shape(shares.shape, BF16), [shares])
    sums = lax.all_to_all(sums, "blk", 0, 0, tiled=True).reshape(512, 2 * rank)
    moment_rows = first + (steps - 2) * held + pulses
    used = -(-moment_rows // 64) * 16
    place = jnp.stack([lax.axis_index("region"), device % 2]).astype(jnp.int32)
    halves = call(halves_kernel, shape((regions, used + 2 * rank, 2 * rank), BF16), [sums, coupling], [place])
    halves = lax.all_to_all(halves, "region", 0, 0, tiled=True)
    others = swap_cores(halves)

    currents = call(
        functools.partial(finish_kernel, steps, farp),
        shape((steps, blocks, pulses, rows), BF16),
        [halves, others, *pays, loc],
        [place],
        scratch=[
            pltpu.VMEM((regions, 2 * used, 2 * rank), BF16),
            pltpu.VMEM((regions, 4 * rank, 2 * rank), BF16),
            pltpu.VMEM(((depth + steps) * regions, pulses, 2 * rank), BF16),
            pltpu.VMEM(((depth + steps) * regions, pulses, 2 * rank), BF16),
            pltpu.VMEM((regions, steps * rank, rank), BF16),
            pltpu.VMEM((regions, 8 * rank, rank), BF16),
            pltpu.VMEM((regions, pulses, steps * rank), BF16),
            pltpu.VMEM((steps * pulses, steps * rank), BF16),
            pltpu.VMEM((2 * regions, 128), jnp.int32),
            pltpu.SMEM((2 * regions, 128), jnp.int32),
            pltpu.SemaphoreType.DMA,
        ],
    )
    return currents[:, None]


def solution(mesh):
    in_specs = (
        P(None, "region", "blk", None, None),
        P(None, "region", "blk", None, None),
        P("region", "blk", None, None),
        P("region", "blk", None, None, None),
        P("region", "blk", None),
        P("region", "blk", None),
        P("region", None),
        P("region", "blk", None, None),
        P("region", "blk", None, None),
        P("region", None),
        P("region", None),
        P("region", None, None, None),
    )
    out_specs = P(None, "region", "blk", None, None)
    return jax.shard_map(on_device, mesh=mesh, in_specs=in_specs, out_specs=out_specs, check_vma=False)
```
